256 devices in a mesh: row: 16 (over y, x), col: 16 (over z, core).
Axes of the slice: x: 4, y: 4, z: 8, core: 2. Of those that a mesh axis runs over, the one named last changes fastest.
Arguments:
- source_points: float32 [24576, 128], P('row'), may hold values from -6 to 6
- target_points: float32 [24576, 128], P('col'), may hold values from -6 to 6
- source_pot: float32 [24576], P('row'), may hold values from -2 to 65
- target_pot: float32 [24576], P('col'), may hold values from -2 to 65
- source_cot: float32 [24576], P('row'), may hold values from -6 to 6
- target_cot: float32 [24576], P('col'), may hold values from -6 to 6
Outputs:
- grad_source: float32 [24576, 128], P(('row', 'col'))
- grad_target: float32 [24576, 128], P(('col', 'row'))
The draws below stay inside these ranges and needn't reach their ends.
All inputs are finite; a program needn't handle non-finite values.
Results may differ from the reference program's by a relative error of at most 0.0003.
Values sent between devices are 32-bit elements; how exact they have to be, the bound alone decides.
A program may use at most 128 MiB of HBM per device.

```python
import jax
import jax.numpy as jnp
from jax import lax

D = 128
PTS_DEV = 1536
ITERS = 3
SOURCES = 24576
TARGETS = 24576


def cloud(key, count_rows):
    shape_key = jax.random.fold_in(key, 0)
    points = jnp.clip(jax.random.normal(shape_key, (count_rows, D), jnp.float32), -6.0, 6.0) * 0.25
    return points


def draw_source_points(key, part):
    key = jax.random.fold_in(key, 11)
    return cloud(key, SOURCES)


def draw_target_points(key, part):
    key = jax.random.fold_in(key, 12)
    return cloud(key, TARGETS)


def draw_source_pot(key, part):
    key = jax.random.fold_in(key, 13)
    return jnp.clip(jax.random.normal(key, (SOURCES,), jnp.float32), -4.0, 4.0) * 0.5


def draw_target_pot(key, part):
    key = jax.random.fold_in(key, 14)
    return jnp.clip(jax.random.normal(key, (TARGETS,), jnp.float32), -4.0, 4.0) * 0.5


def shard_levels(rng, extent, cuts, smallest, high):
    def one(dim, parts):
        draws = jax.random.uniform(jax.random.fold_in(jax.random.fold_in(rng, 6), dim), (parts,), jnp.float32, smallest / len(cuts), high / len(cuts))
        return jnp.repeat(jnp.exp(draws), extent[dim] // parts).reshape((-1,) + (1,) * (len(extent) - dim - 1))

    level = one(*cuts[0])
    for cut in cuts[1:]:
        level = level * one(*cut)
    return level


def noise(key, dims, scale, bound, shards=(), held_as=jnp.bfloat16):
    drawn = scale * jax.random.normal(key, dims, jnp.float32)
    if shards:
        drawn = drawn * shard_levels(key, dims, shards, -0.22, 0.18)
    return jnp.clip(drawn, -bound, bound).astype(held_as)


def setup_inputs(seed: int = 0) -> dict:
    key_list = jax.random.split(jax.random.key(seed), 7)
    source_points = draw_source_points(jax.random.fold_in(key_list[6], 71), 0)
    target_points = draw_target_points(jax.random.fold_in(key_list[6], 71), 0)
    source_pot = draw_source_pot(jax.random.fold_in(key_list[6], 71), 0)
    target_pot = draw_target_pot(jax.random.fold_in(key_list[6], 71), 0)
    source_cot = noise(key_list[4], (SOURCES,), 1.0, 6.0, ((0, 16),), jnp.float32)
    target_cot = noise(key_list[5], (TARGETS,), 1.0, 6.0, ((0, 16),), jnp.float32)
    return {"source_points": source_points, "target_points": target_points, "source_pot": source_pot, "target_pot": target_pot, "source_cot": source_cot, "target_cot": target_cot}


epsilon = 0.5


def pair_distance(query, others):
    inner = lax.dot_general(query, others, (((1,), (1,)), ((), ())), precision=lax.Precision.HIGHEST, preferred_element_type=jnp.float32)
    return 0.5 * jnp.sum(query * query, axis=1)[:, None] + 0.5 * jnp.sum(others * others, axis=1)[None, :] - inner


def blockwise(function, arrays):
    total_rows = arrays[0].shape[0]
    count_blocks = total_rows // PTS_DEV
    shaped = tuple(member.reshape((count_blocks, PTS_DEV) + member.shape[1:]) for member in arrays)
    result = lax.map(lambda packed: function(*packed), shaped)
    return result.reshape((total_rows,) + result.shape[2:])


def log_norms(query, others, other_pot):
    def single(block):
        logits = (other_pot[None, :] - pair_distance(block, others)) / epsilon
        peak = jnp.max(logits, axis=1)
        return peak + jnp.log(jnp.sum(jnp.exp(logits - peak[:, None]), axis=1))
    return blockwise(single, (query,))


def kernel_apply(query, query_pot, others, other_norm, weights):
    def single(block, block_pot):
        kernel = jnp.exp((block_pot[:, None] - pair_distance(block, others)) / epsilon - other_norm[None, :])
        return jnp.dot(kernel, weights, precision=lax.Precision.HIGHEST, preferred_element_type=jnp.float32)
    return blockwise(single, (query, query_pot))


def gradient(query, query_adj, query_pot, query_norm, others, other_adj, other_pot, other_norm):
    def single(block, block_adj, block_pot, block_norm):
        distance = pair_distance(block, others)
        weight = block_adj[:, None] * jnp.exp((other_pot[None, :] - distance) / epsilon - block_norm[:, None])
        weight = weight + other_adj[None, :] * jnp.exp((block_pot[:, None] - distance) / epsilon - other_norm[None, :])
        moved = jnp.dot(weight, others, precision=lax.Precision.HIGHEST, preferred_element_type=jnp.float32)
        return block * jnp.sum(weight, axis=1)[:, None] - moved
    return blockwise(single, (query, query_adj, query_pot, query_norm))


def reference(source_points, target_points, source_pot, target_pot, source_cot, target_cot):
    row_norm = log_norms(source_points, target_points, target_pot)
    col_norm = log_norms(target_points, source_points, source_pot)
    source_adj = source_cot
    target_adj = target_cot
    for iteration in range(ITERS):
        target_adj = target_cot - kernel_apply(target_points, target_pot, source_points, row_norm, source_adj)
        source_adj = source_cot - kernel_apply(source_points, source_pot, target_points, col_norm, target_adj)
    grad_source = gradient(source_points, source_adj, source_pot, row_norm, target_points, target_adj, target_pot, col_norm)
    grad_target = gradient(target_points, target_adj, target_pot, col_norm, source_points, source_adj, source_pot, row_norm)
    return grad_source, grad_target
```

```python
import functools

import jax
import jax.numpy as jnp
from jax import lax
from jax.experimental import pallas as pl
from jax.experimental.pallas import tpu as pltpu
from jax.sharding import PartitionSpec as P

MESH = pl.DeviceIdType.MESH
F32 = jnp.float32
BF16 = jnp.bfloat16
LOG2E = 1.4426950408889634
D = 128
NT = (((1,), (1,)), ((), ()))
NN = (((1,), (0,)), ((), ()))


def mm(left, right, dims):
    return lax.dot_general(left, right, dims, preferred_element_type=F32)


def split(value):
    high = value.astype(BF16)
    return high, (value - high.astype(F32)).astype(BF16)


def column(row):
    return jnp.broadcast_to(row, (128, 128)).T


def kernel(
    nr, nc, cb, lane_chunk,
    x_ref, y_ref, f_ref, g_ref, sc_ref, tc_ref, gs_ref, gt_ref,
    xc, yc, rt, s, rt_hi, rt_lo, s_hi, s_lo, xt, yt, xt2, yt2, scaled,
    peak, coef, send, recv, ssem, rsem,
    ry, ry_pair, ry_send, ry_recv, sx, sx_recv,
    zp, zp_pair, zp_send, zp_recv, tp, tp_recv, cols,
    bulk_s, bulk_r, late_s, late_r,
):
    size = x_ref.shape[0]
    groups = size // 128
    chunks = size // lane_chunk
    wide = lane_chunk // 128
    sub_r, sub_c = size // nr, size // nc
    r, c = lax.axis_index("row"), lax.axis_index("col")
    z, h = c // 2, lax.rem(c, 2)

    barrier = pltpu.get_barrier_semaphore()
    for d in range(1, nr):
        pl.semaphore_signal(barrier, inc=1, device_id=(lax.rem(r + d, nr), c), device_id_type=MESH)
    for d in range(1, nc):
        pl.semaphore_signal(barrier, inc=1, device_id=(r, lax.rem(c + d, nc)), device_id_type=MESH)

    lane = lax.broadcasted_iota(jnp.int32, (128, 128), 1)

    def prepare(k, _):
        rows = pl.ds(pl.multiple_of(k * 128, 128), 128)
        for ref, pot, cat, scale, first, order in (
            (x_ref, f_ref, xc, 2.0 * LOG2E, 0, (0, 1, 0)),
            (y_ref, g_ref, yc, 1.0, 3, (0, 0, 1)),
        ):
            tile = ref[rows, :]
            parts = split(tile * scale)
            for slot, which in enumerate(order):
                cat[rows, slot * D:(slot + 1) * D] = parts[which]
            norm = jnp.sum(tile * tile, axis=1, keepdims=True)
            offset = LOG2E * (2.0 * column(pot[pl.ds(k, 1), :]) - norm)
            one = offset.astype(BF16).astype(F32)
            two = (offset - one).astype(BF16).astype(F32)
            three = offset - one - two
            extra = jnp.where(lane < 6, 1.0, 0.0)
            for place, piece in enumerate((one, two, three)):
                extra = jnp.where(lane == first + place, piece, extra)
            cat[rows, 3 * D:] = extra.astype(BF16)
        return 0

    lax.fori_loop(0, groups, prepare, 0)

    def soften(left, right, out, peak_slot, round_slot):
        tall = 256 if size % 256 == 0 else 128

        def one(k, _):
            lanes = pl.ds(pl.multiple_of(k * lane_chunk, lane_chunk), lane_chunk)
            rhs = right[lanes, :]

            def logits(q, top):
                rows = pl.ds(pl.multiple_of(q * tall, tall), tall)
                tile = mm(left[rows, :], rhs, NT)
                out[rows, lanes] = tile
                return jnp.maximum(top, jnp.max(tile.reshape(tall // 8, 8, lane_chunk), axis=0))

            top = lax.fori_loop(0, size // tall, logits, jnp.full((8, lane_chunk), -jnp.inf, F32), unroll=True)
            top = jnp.max(top, axis=0, keepdims=True)

            def weights(q, total):
                rows = pl.ds(pl.multiple_of(q * 64, 64), 64)
                tile = jnp.exp2(out[rows, lanes] - top)
                out[rows, lanes] = tile
                return total + jnp.sum(tile.reshape(8, 8, lane_chunk), axis=0)

            total = lax.fori_loop(0, size // 64, weights, jnp.zeros((8, lane_chunk), F32))
            total = jnp.sum(total, axis=0, keepdims=True)
            local = top + LOG2E * jnp.log(total)
            for w in range(wide):
                peak[peak_slot, pl.ds(k * wide + w, 1), :] = top[:, w * 128:(w + 1) * 128]
                send[round_slot, pl.ds(k * wide + w, 1), :] = local[:, w * 128:(w + 1) * 128]
            return 0

        lax.fori_loop(0, chunks, one, 0)

    def exchange(slot, along_row):
        n = nr if along_row else nc
        order = sorted(range(1, n), key=lambda d: -min(d, n - d))
        for d in order:
            device = (lax.rem(r + d, n), c) if along_row else (r, lax.rem(c + d, n))
            pltpu.make_async_remote_copy(
                send.at[slot], recv.at[slot, d - 1], ssem.at[slot], rsem.at[slot],
                device_id=device, device_id_type=MESH,
            ).start()

    def wait_bytes(ref, sem):
        pltpu.make_async_copy(ref, ref, sem).wait()

    def arrived(slot, n):
        wait_bytes(recv.at[slot, pl.ds(0, n - 1)], rsem.at[slot])

    def total_of(slot, n):
        total = send[slot]
        for d in range(n - 1):
            total = total + recv[slot, d]
        return total

    def norm_scale(slot, n, peak_slot):
        top = send[slot]
        for d in range(n - 1):
            top = jnp.maximum(top, recv[slot, d])
        total = jnp.exp2(send[slot] - top)
        for d in range(n - 1):
            total = total + jnp.exp2(recv[slot, d] - top)
        return jnp.exp2(peak[peak_slot] - top - LOG2E * jnp.log(total))

    def matvec(matrix, slot):
        def one(k, _):
            rows = pl.ds(pl.multiple_of(k * 128, 128), 128)
            acc = matrix[rows, 0:128] * coef[0:1, :]
            for q in range(1, groups):
                acc = acc + matrix[rows, q * 128:(q + 1) * 128] * coef[q:q + 1, :]
            send[slot, pl.ds(k, 1), :] = jnp.sum(acc.T, axis=0, keepdims=True)
            return 0

        lax.fori_loop(0, groups, one, 0)

    def halves(matrix, high, low):
        def one(k, _):
            rows = pl.ds(pl.multiple_of(k * 32, 32), 32)
            high[rows, :], low[rows, :] = split(matrix[rows, :])
            return 0

        lax.fori_loop(0, size // 32, one, 0)

    def turned(ref, out, out2):
        for k in range(groups):
            lanes = slice(k * 128, (k + 1) * 128)
            tile = ref[lanes, :].T
            out[:, lanes] = tile
            out2[0:D, lanes], out2[D:2 * D, lanes] = split(tile)

    def early(points2, high, low, scale, out):
        for k in range(chunks):
            lanes = slice(k * lane_chunk, (k + 1) * lane_chunk)
            both = mm(points2[...], high[:, lanes], NN)
            tile = both[0:D] + both[D:2 * D] + mm(points2[0:D, :], low[:, lanes], NN)
            for w in range(wide):
                group = k * wide + w
                block = tile[:, w * 128:(w + 1) * 128] * scale[group:group + 1, :]
                out[group * 128:(group + 1) * 128, :] = block.T

    def scale_points(points):
        for k in range(groups):
            lanes = slice(k * 128, (k + 1) * 128)
            scaled[0:D, lanes], scaled[D:2 * D, lanes] = split(points[:, lanes] * coef[k:k + 1, :])

    half = cb // 2
    ch_c, ch_r = nc // cb, nr // cb

    def offsets(n):
        return sorted(range(n), key=lambda o: -min(o, n - o))

    def z_dest(o, t):
        return lax.rem(z // half + o, ch_c) * half + lax.rem(z + t, half)

    def r_dest(o, t):
        return lax.rem(r // cb + o, ch_r) * cb + lax.rem(r + t, cb)

    z_list = [(o, t) for o in offsets(ch_c) for t in reversed(range(half))]
    r_list = [(o, t) for o in offsets(ch_r) for t in reversed(range(cb))]

    def block(index, rows):
        return pl.ds(pl.multiple_of(index * rows, 8), rows)

    def to_partner(source, pair, slot, o, t, s_sem, r_sem):
        pltpu.make_async_remote_copy(
            source.at[block(z_dest(o, t) * 2 + 1 - h, sub_c)], pair.at[slot], s_sem, r_sem,
            device_id=(r, z * 2 + 1 - h), device_id_type=MESH,
        ).start()

    def along_z(out, inbox, slot, o, t, s_sem, r_sem):
        pltpu.make_async_remote_copy(
            out.at[slot], inbox.at[slot], s_sem, r_sem,
            device_id=(r, z_dest(o, t) * 2 + h), device_id_type=MESH,
        ).start()

    def along_r(source, inbox, slot, o, t, s_sem, r_sem):
        pltpu.make_async_remote_copy(
            source.at[block(r_dest(o, t), sub_r)], inbox.at[slot], s_sem, r_sem,
            device_id=(r_dest(o, t), c), device_id_type=MESH,
        ).start()

    nz = nc // 2

    soften(yc, xc, rt, 0, 0)
    pl.semaphore_wait(barrier, nr + nc - 2)
    exchange(0, False)
    soften(xc, yc, s, 1, 1)
    exchange(1, True)
    turned(y_ref, yt, yt2)
    turned(x_ref, xt, xt2)
    arrived(0, nc)
    rho = norm_scale(0, nc, 0)

    coef[...] = rho * sc_ref[...]
    matvec(rt, 2)
    exchange(2, True)
    halves(rt, rt_hi, rt_lo)
    early(yt2, rt_hi, rt_lo, rho, ry)
    for slot, (o, t) in enumerate(z_list):
        to_partner(ry, ry_pair, slot, o, t, bulk_s.at[0], bulk_r.at[0])
    arrived(1, nr)
    sigma = norm_scale(1, nr, 1)
    arrived(2, nr)
    target_adj = tc_ref[...] - total_of(2, nr)

    coef[...] = sigma * target_adj
    matvec(s, 3)
    exchange(3, False)
    halves(s, s_hi, s_lo)
    wait_bytes(ry_pair, bulk_r.at[0])
    for slot, (o, t) in enumerate(z_list):
        ry_send[slot] = ry[block(z_dest(o, t) * 2 + h, sub_c), :] + ry_pair[slot]
    arrived(3, nc)
    source_adj = sc_ref[...] - total_of(3, nc)

    coef[...] = rho * source_adj
    matvec(rt, 4)
    exchange(4, True)
    cut = nz // 2
    for slot in range(cut):
        along_z(ry_send, ry_recv, slot, *z_list[slot], bulk_s.at[1], bulk_r.at[1])
    early(xt2, s_hi, s_lo, sigma, sx)
    arrived(4, nr)
    target_adj = tc_ref[...] - total_of(4, nr)

    coef[...] = sigma * target_adj
    matvec(s, 5)
    exchange(5, False)
    for slot, (o, t) in enumerate(r_list[:-1]):
        along_r(sx, sx_recv, slot, o, t, bulk_s.at[3], bulk_r.at[3])
    arrived(5, nc)
    source_adj = sc_ref[...] - total_of(5, nc)

    coef[...] = rho * source_adj
    matvec(rt, 6)
    exchange(6, True)
    for slot in range(cut, nz - 1):
        along_z(ry_send, ry_recv, slot, *z_list[slot], bulk_s.at[2], bulk_r.at[2])
    arrived(6, nr)
    target_adj = tc_ref[...] - total_of(6, nr)

    coef[...] = sigma * target_adj
    matvec(s, 7)
    exchange(7, False)
    scale_points(yt)
    tall_c = cb * sub_c

    def z_forward(n):
        wait_bytes(zp_pair.at[pl.ds(n * half, half)], late_r.at[n])
        for slot in range(n * half, (n + 1) * half):
            o, t = z_list[slot]
            zp_send[slot] = zp[block(z_dest(o, t) * 2 + h, sub_c), :] + zp_pair[slot]
            if slot < nz - 1:
                along_z(zp_send, zp_recv, slot, o, t, late_s.at[ch_c], late_r.at[ch_c])

    for n in range(ch_c):
        rows = block(lax.rem(z // half + z_list[n * half][0], ch_c), tall_c)
        both = mm(s_hi[rows, :], scaled[...], NT)
        zp[rows, :] = both[:, 0:D] + both[:, D:2 * D] + mm(s_lo[rows, :], scaled[0:D, :], NT)
        for slot in range(n * half, (n + 1) * half):
            to_partner(zp, zp_pair, slot, *z_list[slot], late_s.at[n], late_r.at[n])
        if n:
            z_forward(n - 1)
    z_forward(ch_c - 1)

    arrived(7, nc)
    source_adj = sc_ref[...] - total_of(7, nc)

    coef[...] = rho * source_adj
    scale_points(xt)
    tall_r = cb * sub_r
    for n in range(ch_r):
        rows = block(lax.rem(r // cb + r_list[n * cb][0], ch_r), tall_r)
        both = mm(rt_hi[rows, :], scaled[...], NT)
        moved = both[:, 0:D] + both[:, D:2 * D] + mm(rt_lo[rows, :], scaled[0:D, :], NT)
        acc = rt[rows, 0:128] * coef[0:1, :]
        for q in range(1, groups):
            acc = acc + rt[rows, q * 128:(q + 1) * 128] * coef[q:q + 1, :]
        tp[rows, :] = y_ref[rows, :] * jnp.sum(acc, axis=1, keepdims=True) - moved
        for slot in range(n * cb, (n + 1) * cb):
            if slot < nr - 1:
                along_r(tp, tp_recv, slot, *r_list[slot], late_s.at[ch_c + 1], late_r.at[ch_c + 1])

    for k in range(groups):
        rows = slice(k * 128, (k + 1) * 128)
        cols[0, rows, :] = column(sc_ref[k:k + 1, :])
        cols[1, rows, :] = column(source_adj[k:k + 1, :])
        cols[2, rows, :] = column(target_adj[k:k + 1, :])

    own_c, own_r = block(c, sub_c), block(r, sub_r)
    wait_bytes(ry_recv.at[pl.ds(0, cut)], bulk_r.at[1])
    wait_bytes(ry_recv.at[pl.ds(cut, nz - 1 - cut)], bulk_r.at[2])
    moved = ry_send[nz - 1]
    for slot in range(nz - 1):
        moved = moved + ry_recv[slot]
    wait_bytes(sx_recv, bulk_r.at[3])
    other = sx[own_r, :]
    for slot in range(nr - 1):
        other = other + sx_recv[slot]
    wait_bytes(zp_recv, late_r.at[ch_c])
    late = zp_send[nz - 1]
    for slot in range(nz - 1):
        late = late + zp_recv[slot]
    gs_ref[...] = x_ref[own_c, :] * cols[0, own_c, :] - cols[1, own_c, :] * moved - late
    wait_bytes(tp_recv, late_r.at[ch_c + 1])
    late = tp[own_r, :]
    for slot in range(nr - 1):
        late = late + tp_recv[slot]
    gt_ref[...] = cols[2, own_r, :] * (y_ref[own_r, :] - other) + late

    for slot, n in enumerate((nc, nr, nr, nc, nr, nc, nr, nc)):
        wait_bytes(recv.at[slot, pl.ds(0, n - 1)], ssem.at[slot])
    wait_bytes(ry_pair, bulk_s.at[0])
    wait_bytes(ry_recv.at[pl.ds(0, cut)], bulk_s.at[1])
    wait_bytes(ry_recv.at[pl.ds(cut, nz - 1 - cut)], bulk_s.at[2])
    wait_bytes(sx_recv, bulk_s.at[3])
    for n in range(ch_c):
        wait_bytes(zp_pair.at[pl.ds(n * half, half)], late_s.at[n])
    wait_bytes(zp_recv, late_s.at[ch_c])
    wait_bytes(tp_recv, late_s.at[ch_c + 1])


def shards(nr, nc, cb, lane_chunk, x, y, f, g, sc, tc):
    size = x.shape[0]
    groups = size // 128
    sub_r, sub_c = size // nr, size // nc
    vectors = [v.reshape(groups, 128) for v in (f, g, sc, tc)]
    vmem = pl.BlockSpec(memory_space=pltpu.VMEM)
    peers = max(nr, nc) - 1
    nz = nc // 2
    square = (size, size)
    return pl.pallas_call(
        functools.partial(kernel, nr, nc, cb, lane_chunk),
        out_shape=(
            jax.ShapeDtypeStruct((sub_c, D), F32),
            jax.ShapeDtypeStruct((sub_r, D), F32),
        ),
        in_specs=[vmem] * 6,
        out_specs=(vmem, vmem),
        scratch_shapes=[
            pltpu.VMEM((size, 4 * D), BF16),
            pltpu.VMEM((size, 4 * D), BF16),
            pltpu.VMEM(square, F32),
            pltpu.VMEM(square, F32),
            pltpu.VMEM(square, BF16),
            pltpu.VMEM(square, BF16),
            pltpu.VMEM(square, BF16),
            pltpu.VMEM(square, BF16),
            pltpu.VMEM((D, size), F32),
            pltpu.VMEM((D, size), F32),
            pltpu.VMEM((2 * D, size), BF16),
            pltpu.VMEM((2 * D, size), BF16),
            pltpu.VMEM((2 * D, size), BF16),
            pltpu.VMEM((2, groups, 128), F32),
            pltpu.VMEM((groups, 128), F32),
            pltpu.VMEM((8, groups, 128), F32),
            pltpu.VMEM((8, peers, groups, 128), F32),
            pltpu.SemaphoreType.DMA((8,)),
            pltpu.SemaphoreType.DMA((8,)),
            pltpu.VMEM((size, D), F32),
            pltpu.VMEM((nz, sub_c, D), F32),
            pltpu.VMEM((nz, sub_c, D), F32),
            pltpu.VMEM((nz - 1, sub_c, D), F32),
            pltpu.VMEM((size, D), F32),
            pltpu.VMEM((nr - 1, sub_r, D), F32),
            pltpu.VMEM((size, D), F32),
            pltpu.VMEM((nz, sub_c, D), F32),
            pltpu.VMEM((nz, sub_c, D), F32),
            pltpu.VMEM((nz - 1, sub_c, D), F32),
            pltpu.VMEM((size, D), F32),
            pltpu.VMEM((nr - 1, sub_r, D), F32),
            pltpu.VMEM((3, size, D), F32),
            pltpu.SemaphoreType.DMA((4,)),
            pltpu.SemaphoreType.DMA((4,)),
            pltpu.SemaphoreType.DMA((nc // cb + 2,)),
            pltpu.SemaphoreType.DMA((nc // cb + 2,)),
        ],
        compiler_params=pltpu.CompilerParams(
            collective_id=0, has_side_effects=True, vmem_limit_bytes=62 << 20
        ),
    )(x, y, *vectors)


def solution(mesh, cb=4, lane_chunk=256):
    in_specs = (P("row", None), P("col", None), P("row"), P("col"), P("row"), P("col"))
    out_specs = (P(("row", "col"), None), P(("col", "row"), None))
    body = functools.partial(shards, mesh.shape["row"], mesh.shape["col"], cb, lane_chunk)
    return jax.shard_map(body, mesh=mesh, in_specs=in_specs, out_specs=out_specs, check_vma=False)
```

```python
import functools

import jax
import jax.numpy as jnp
from jax import lax
from jax.experimental import pallas as pl
from jax.experimental.pallas import tpu as pltpu
from jax.sharding import PartitionSpec as P

MESH = pl.DeviceIdType.MESH
F32 = jnp.float32
BF16 = jnp.bfloat16
LOG2E = 1.4426950408889634
D = 128
NT = (((1,), (1,)), ((), ()))
NN = (((1,), (0,)), ((), ()))


def mm(left, right, dims):
    return lax.dot_general(left, right, dims, preferred_element_type=F32)


def split(value):
    high = value.astype(BF16)
    return high, (value - high.astype(F32)).astype(BF16)


def column(row):
    return jnp.broadcast_to(row, (128, 128)).T


def kernel(
    nr, nc, cb, lane_chunk, pieces,
    x_ref, y_ref, f_ref, g_ref, sc_ref, tc_ref, gs_ref, gt_ref,
    xc, yc, rt, s, rt_hi, rt_lo, s_hi, s_lo, xt, yt, xt2, yt2, scaled,
    peak, coef, send, recv, ssem, rsem,
    ry, ry_pair, ry_send, ry_recv, sx,
    zp, zp_pair, zp_send, zp_recv, tp, tp_recv, cols,
    bulk_s, bulk_r, late_s, late_r,
):
    size = x_ref.shape[0]
    groups = size // 128
    chunks = size // lane_chunk
    wide = lane_chunk // 128
    per = groups // pieces
    sub_r, sub_c = size // nr, size // nc
    r, c = lax.axis_index("row"), lax.axis_index("col")
    z, h = c // 2, lax.rem(c, 2)

    barrier = pltpu.get_barrier_semaphore()
    for d in range(1, nr):
        pl.semaphore_signal(barrier, inc=1, device_id=(lax.rem(r + d, nr), c), device_id_type=MESH)
    for d in range(1, nc):
        pl.semaphore_signal(barrier, inc=1, device_id=(r, lax.rem(c + d, nc)), device_id_type=MESH)

    lane = lax.broadcasted_iota(jnp.int32, (128, 128), 1)

    def prepare(k):
        rows = slice(k * 128, (k + 1) * 128)
        for ref, pot, cat, scale, first, order in (
            (x_ref, f_ref, xc, 2.0 * LOG2E, 0, (0, 1, 0)),
            (y_ref, g_ref, yc, 1.0, 3, (0, 0, 1)),
        ):
            tile = ref[rows, :]
            parts = split(tile * scale)
            for slot, which in enumerate(order):
                cat[rows, slot * D:(slot + 1) * D] = parts[which]
            norm = jnp.sum(tile * tile, axis=1, keepdims=True)
            offset = LOG2E * (2.0 * column(pot[k:k + 1, :]) - norm)
            one = offset.astype(BF16).astype(F32)
            two = (offset - one).astype(BF16).astype(F32)
            three = offset - one - two
            extra = jnp.where(lane < 6, 1.0, 0.0)
            for place, piece in enumerate((one, two, three)):
                extra = jnp.where(lane == first + place, piece, extra)
            cat[rows, 3 * D:] = extra.astype(BF16)

    for k in range(groups):
        prepare(k)

    def soften(left, right, out, peak_slot, round_slot, along_row):
        tall = 256 if size % 256 == 0 else 128
        tops = []
        for k in range(chunks + 1):
            top = jnp.full((8, lane_chunk), -jnp.inf, F32)
            total = jnp.zeros((8, lane_chunk), F32)
            ahead = slice(k * lane_chunk, (k + 1) * lane_chunk)
            lanes = slice((k - 1) * lane_chunk, k * lane_chunk)
            for q in range(size // tall):
                rows = slice(q * tall, (q + 1) * tall)
                if k < chunks:
                    tile = mm(left[rows, :], right[ahead, :], NT)
                    out[rows, ahead] = tile
                    top = jnp.maximum(top, jnp.max(tile.reshape(tall // 8, 8, lane_chunk), axis=0))
                if k:
                    tile = jnp.exp2(out[rows, lanes] - tops[k - 1])
                    out[rows, lanes] = tile
                    total = total + jnp.sum(tile.reshape(tall // 8, 8, lane_chunk), axis=0)
            if k < chunks:
                tops.append(jnp.max(top, axis=0, keepdims=True))
            if k:
                total = jnp.sum(total, axis=0, keepdims=True)
                local = tops[k - 1] + LOG2E * jnp.log(total)
                for w in range(wide):
                    group, part = (k - 1) * wide + w, slice(w * 128, (w + 1) * 128)
                    peak[peak_slot, group:group + 1, :] = tops[k - 1][:, part]
                    send[round_slot, group:group + 1, :] = local[:, part]
                    if (group + 1) % per == 0:
                        if group + 1 == per and not along_row:
                            pl.semaphore_wait(barrier, nr + nc - 2)
                        exchange(round_slot, along_row, group + 1 - per)

    def exchange(slot, along_row, first):
        n = nr if along_row else nc
        order = sorted(range(1, n), key=lambda d: -min(d, n - d))
        for d in order:
            device = (lax.rem(r + d, n), c) if along_row else (r, lax.rem(c + d, n))
            pltpu.make_async_remote_copy(
                send.at[slot, pl.ds(first, per)], recv.at[slot, d - 1, pl.ds(first, per)],
                ssem.at[slot], rsem.at[slot], device_id=device, device_id_type=MESH,
            ).start()

    def wait_bytes(ref, sem):
        pltpu.make_async_copy(ref, ref, sem).wait()

    def arrived(slot, n):
        wait_bytes(recv.at[slot, pl.ds(0, n - 1)], rsem.at[slot])

    def total_of(slot, n):
        total = send[slot]
        for d in range(n - 1):
            total = total + recv[slot, d]
        return total

    def norm_scale(slot, n, peak_slot):
        top = send[slot]
        for d in range(n - 1):
            top = jnp.maximum(top, recv[slot, d])
        total = jnp.exp2(send[slot] - top)
        for d in range(n - 1):
            total = total + jnp.exp2(recv[slot, d] - top)
        return jnp.exp2(peak[peak_slot] - top - LOG2E * jnp.log(total))

    def push(matrix, slot, along_row):
        for k in range(groups):
            rows = slice(k * 128, (k + 1) * 128)
            acc = matrix[rows, 0:128] * coef[0:1, :]
            for q in range(1, groups):
                acc = acc + matrix[rows, q * 128:(q + 1) * 128] * coef[q:q + 1, :]
            send[slot, k:k + 1, :] = jnp.sum(acc.T, axis=0, keepdims=True)
            if (k + 1) % per == 0:
                exchange(slot, along_row, k + 1 - per)

    def halves(matrix, high, low):
        def one(k, _):
            rows = pl.ds(pl.multiple_of(k * 32, 32), 32)
            high[rows, :], low[rows, :] = split(matrix[rows, :])
            return 0

        lax.fori_loop(0, size // 32, one, 0)

    def turned(ref, out, out2):
        for k in range(groups):
            lanes = slice(k * 128, (k + 1) * 128)
            tile = ref[lanes, :].T
            out[:, lanes] = tile
            out2[0:D, lanes], out2[D:2 * D, lanes] = split(tile)

    def early(points2, high, low, scale, out):
        for k in range(chunks):
            lanes = slice(k * lane_chunk, (k + 1) * lane_chunk)
            both = mm(points2[...], high[:, lanes], NN)
            tile = both[0:D] + both[D:2 * D] + mm(points2[0:D, :], low[:, lanes], NN)
            for w in range(wide):
                group = k * wide + w
                block = tile[:, w * 128:(w + 1) * 128] * scale[group:group + 1, :]
                out[group * 128:(group + 1) * 128, :] = block.T

    def fill_column(slot, rows_of):
        for k in range(groups):
            cols[slot, k * 128:(k + 1) * 128, :] = column(rows_of[k:k + 1, :])

    def scale_points(points):
        for k in range(groups):
            lanes = slice(k * 128, (k + 1) * 128)
            scaled[0:D, lanes], scaled[D:2 * D, lanes] = split(points[:, lanes] * coef[k:k + 1, :])

    half = cb // 2
    ch_c, ch_r = nc // cb, nr // cb

    def offsets(n):
        return sorted(range(n), key=lambda o: -min(o, n - o))

    def z_dest(o, t):
        return lax.rem(z // half + o, ch_c) * half + lax.rem(z + t, half)

    def r_dest(o, t):
        return lax.rem(r // cb + o, ch_r) * cb + lax.rem(r + t, cb)

    z_list = [(o, t) for o in offsets(ch_c) for t in reversed(range(half))]
    r_list = [(o, t) for o in offsets(ch_r) for t in reversed(range(cb))]

    def block(index, rows):
        return pl.ds(pl.multiple_of(index * rows, 8), rows)

    def to_partner(source, pair, slot, o, t, s_sem, r_sem):
        pltpu.make_async_remote_copy(
            source.at[block(z_dest(o, t) * 2 + 1 - h, sub_c)], pair.at[slot], s_sem, r_sem,
            device_id=(r, z * 2 + 1 - h), device_id_type=MESH,
        ).start()

    def along_z(out, inbox, slot, o, t, s_sem, r_sem):
        pltpu.make_async_remote_copy(
            out.at[slot], inbox.at[slot], s_sem, r_sem,
            device_id=(r, z_dest(o, t) * 2 + h), device_id_type=MESH,
        ).start()

    def along_r(source, inbox, slot, o, t, s_sem, r_sem):
        pltpu.make_async_remote_copy(
            source.at[block(r_dest(o, t), sub_r)], inbox.at[slot], s_sem, r_sem,
            device_id=(r_dest(o, t), c), device_id_type=MESH,
        ).start()

    nz = nc // 2

    soften(yc, xc, rt, 0, 0, False)
    soften(xc, yc, s, 1, 1, True)
    turned(y_ref, yt, yt2)
    turned(x_ref, xt, xt2)
    arrived(0, nc)
    rho = norm_scale(0, nc, 0)

    coef[...] = rho * sc_ref[...]
    push(rt, 2, True)
    halves(rt, rt_hi, rt_lo)
    early(yt2, rt_hi, rt_lo, rho, ry)
    for slot, (o, t) in enumerate(z_list):
        to_partner(ry, ry_pair, slot, o, t, bulk_s.at[0], bulk_r.at[0])
    arrived(1, nr)
    sigma = norm_scale(1, nr, 1)
    arrived(2, nr)
    target_adj = tc_ref[...] - total_of(2, nr)

    coef[...] = sigma * target_adj
    push(s, 3, False)
    halves(s, s_hi, s_lo)
    wait_bytes(ry_pair, bulk_r.at[0])
    for slot, (o, t) in enumerate(z_list):
        ry_send[slot] = ry[block(z_dest(o, t) * 2 + h, sub_c), :] + ry_pair[slot]
    arrived(3, nc)
    source_adj = sc_ref[...] - total_of(3, nc)

    coef[...] = rho * source_adj
    push(rt, 4, True)
    cut = nz // 2
    for slot in range(cut):
        along_z(ry_send, ry_recv, slot, *z_list[slot], bulk_s.at[1], bulk_r.at[1])
    early(xt2, s_hi, s_lo, sigma, sx)
    arrived(4, nr)
    target_adj = tc_ref[...] - total_of(4, nr)

    coef[...] = sigma * target_adj
    push(s, 5, False)
    fill_column(0, sc_ref)
    arrived(5, nc)
    source_adj = sc_ref[...] - total_of(5, nc)

    coef[...] = rho * source_adj
    push(rt, 6, True)
    for slot in range(cut, nz - 1):
        along_z(ry_send, ry_recv, slot, *z_list[slot], bulk_s.at[2], bulk_r.at[2])
    arrived(6, nr)
    target_adj = tc_ref[...] - total_of(6, nr)

    coef[...] = sigma * target_adj
    push(s, 7, False)
    scale_points(yt)
    tall_c = cb * sub_c

    def z_forward(n):
        wait_bytes(zp_pair.at[pl.ds(n * half, half)], late_r.at[n])
        for slot in range(n * half, (n + 1) * half):
            o, t = z_list[slot]
            zp_send[slot] = zp[block(z_dest(o, t) * 2 + h, sub_c), :] + zp_pair[slot]
            if slot < nz - 1:
                along_z(zp_send, zp_recv, slot, o, t, late_s.at[ch_c], late_r.at[ch_c])

    for n in range(ch_c):
        rows = block(lax.rem(z // half + z_list[n * half][0], ch_c), tall_c)
        both = mm(s_hi[rows, :], scaled[...], NT)
        zp[rows, :] = both[:, 0:D] + both[:, D:2 * D] + mm(s_lo[rows, :], scaled[0:D, :], NT)
        for slot in range(n * half, (n + 1) * half):
            to_partner(zp, zp_pair, slot, *z_list[slot], late_s.at[n], late_r.at[n])
        if n:
            z_forward(n - 1)
    z_forward(ch_c - 1)
    fill_column(2, target_adj)
    sx[...] = sx[...] * cols[2]

    arrived(7, nc)
    source_adj = sc_ref[...] - total_of(7, nc)

    coef[...] = rho * source_adj
    scale_points(xt)
    tall_r = cb * sub_r
    for n in range(ch_r):
        rows = block(lax.rem(r // cb + r_list[n * cb][0], ch_r), tall_r)
        both = mm(rt_hi[rows, :], scaled[...], NT)
        moved = both[:, 0:D] + both[:, D:2 * D] + mm(rt_lo[rows, :], scaled[0:D, :], NT)
        acc = rt[rows, 0:128] * coef[0:1, :]
        for q in range(1, groups):
            acc = acc + rt[rows, q * 128:(q + 1) * 128] * coef[q:q + 1, :]
        tp[rows, :] = y_ref[rows, :] * jnp.sum(acc, axis=1, keepdims=True) - moved - sx[rows, :]
        for slot in range(n * cb, (n + 1) * cb):
            if slot < nr - 1:
                along_r(tp, tp_recv, slot, *r_list[slot], late_s.at[ch_c + 1], late_r.at[ch_c + 1])

    fill_column(1, source_adj)
    own_c, own_r = block(c, sub_c), block(r, sub_r)
    wait_bytes(ry_recv.at[pl.ds(0, cut)], bulk_r.at[1])
    wait_bytes(ry_recv.at[pl.ds(cut, nz - 1 - cut)], bulk_r.at[2])
    moved = ry_send[nz - 1]
    for slot in range(nz - 1):
        moved = moved + ry_recv[slot]
    wait_bytes(zp_recv, late_r.at[ch_c])
    late = zp_send[nz - 1]
    for slot in range(nz - 1):
        late = late + zp_recv[slot]
    gs_ref[...] = x_ref[own_c, :] * cols[0, own_c, :] - cols[1, own_c, :] * moved - late
    wait_bytes(tp_recv, late_r.at[ch_c + 1])
    late = tp[own_r, :]
    for slot in range(nr - 1):
        late = late + tp_recv[slot]
    gt_ref[...] = cols[2, own_r, :] * y_ref[own_r, :] + late

    for slot, n in enumerate((nc, nr, nr, nc, nr, nc, nr, nc)):
        wait_bytes(recv.at[slot, pl.ds(0, n - 1)], ssem.at[slot])
    wait_bytes(ry_pair, bulk_s.at[0])
    wait_bytes(ry_recv.at[pl.ds(0, cut)], bulk_s.at[1])
    wait_bytes(ry_recv.at[pl.ds(cut, nz - 1 - cut)], bulk_s.at[2])
    for n in range(ch_c):
        wait_bytes(zp_pair.at[pl.ds(n * half, half)], late_s.at[n])
    wait_bytes(zp_recv, late_s.at[ch_c])
    wait_bytes(tp_recv, late_s.at[ch_c + 1])


def shards(nr, nc, cb, lane_chunk, pieces, x, y, f, g, sc, tc):
    size = x.shape[0]
    groups = size // 128
    sub_r, sub_c = size // nr, size // nc
    vectors = [v.reshape(groups, 128) for v in (f, g, sc, tc)]
    vmem = pl.BlockSpec(memory_space=pltpu.VMEM)
    peers = max(nr, nc) - 1
    nz = nc // 2
    square = (size, size)
    return pl.pallas_call(
        functools.partial(kernel, nr, nc, cb, lane_chunk, pieces),
        out_shape=(
            jax.ShapeDtypeStruct((sub_c, D), F32),
            jax.ShapeDtypeStruct((sub_r, D), F32),
        ),
        in_specs=[vmem] * 6,
        out_specs=(vmem, vmem),
        scratch_shapes=[
            pltpu.VMEM((size, 4 * D), BF16),
            pltpu.VMEM((size, 4 * D), BF16),
            pltpu.VMEM(square, F32),
            pltpu.VMEM(square, F32),
            pltpu.VMEM(square, BF16),
            pltpu.VMEM(square, BF16),
            pltpu.VMEM(square, BF16),
            pltpu.VMEM(square, BF16),
            pltpu.VMEM((D, size), F32),
            pltpu.VMEM((D, size), F32),
            pltpu.VMEM((2 * D, size), BF16),
            pltpu.VMEM((2 * D, size), BF16),
            pltpu.VMEM((2 * D, size), BF16),
            pltpu.VMEM((2, groups, 128), F32),
            pltpu.VMEM((groups, 128), F32),
            pltpu.VMEM((8, groups, 128), F32),
            pltpu.VMEM((8, peers, groups, 128), F32),
            pltpu.SemaphoreType.DMA((8,)),
            pltpu.SemaphoreType.DMA((8,)),
            pltpu.VMEM((size, D), F32),
            pltpu.VMEM((nz, sub_c, D), F32),
            pltpu.VMEM((nz, sub_c, D), F32),
            pltpu.VMEM((nz - 1, sub_c, D), F32),
            pltpu.VMEM((size, D), F32),
            pltpu.VMEM((size, D), F32),
            pltpu.VMEM((nz, sub_c, D), F32),
            pltpu.VMEM((nz, sub_c, D), F32),
            pltpu.VMEM((nz - 1, sub_c, D), F32),
            pltpu.VMEM((size, D), F32),
            pltpu.VMEM((nr - 1, sub_r, D), F32),
            pltpu.VMEM((3, size, D), F32),
            pltpu.SemaphoreType.DMA((3,)),
            pltpu.SemaphoreType.DMA((3,)),
            pltpu.SemaphoreType.DMA((nc // cb + 2,)),
            pltpu.SemaphoreType.DMA((nc // cb + 2,)),
        ],
        compiler_params=pltpu.CompilerParams(
            collective_id=0, has_side_effects=True, vmem_limit_bytes=62 << 20
        ),
    )(x, y, *vectors)


def solution(mesh, cb=4, lane_chunk=256, pieces=1):
    in_specs = (P("row", None), P("col", None), P("row"), P("col"), P("row"), P("col"))
    out_specs = (P(("row", "col"), None), P(("col", "row"), None))
    body = functools.partial(shards, mesh.shape["row"], mesh.shape["col"], cb, lane_chunk, pieces)
    return jax.shard_map(body, mesh=mesh, in_specs=in_specs, out_specs=out_specs, check_vma=False)
```

```python
import functools

import jax
import jax.numpy as jnp
from jax import lax
from jax.experimental import pallas as pl
from jax.experimental.pallas import tpu as pltpu
from jax.sharding import PartitionSpec as P

MESH = pl.DeviceIdType.MESH
F32 = jnp.float32
BF16 = jnp.bfloat16
LOG2E = 1.4426950408889634
D = 128
NT = (((1,), (1,)), ((), ()))
NN = (((1,), (0,)), ((), ()))


def mm(left, right, dims):
    return lax.dot_general(left, right, dims, preferred_element_type=F32)


def split(value):
    high = value.astype(BF16)
    return high, (value - high.astype(F32)).astype(BF16)


def column(row):
    return jnp.broadcast_to(row, (128, 128)).T


def kernel(
    nr, nc, cb, lane_chunk, pieces,
    x_ref, y_ref, f_ref, g_ref, sc_ref, tc_ref, out_ref,
    xc, yc, rt, s, rt_hi, rt_lo, s_hi, s_lo, xt, yt, xt2, yt2, scaled,
    peak, coef, send, recv, ssem, rsem,
    ry, ry_pair, ry_send, ry_recv, sx,
    zp, zp_pair, zp_send, zp_recv, tp, tp_recv, cols,
    bulk_s, bulk_r, late_s, late_r,
):
    size = x_ref.shape[0]
    groups = size // 128
    chunks = size // lane_chunk
    wide = lane_chunk // 128
    per = groups // pieces
    sub_r, sub_c = size // nr, size // nc
    r, c = lax.axis_index("row"), lax.axis_index("col")
    z, h = c // 2, lax.rem(c, 2)

    barrier = pltpu.get_barrier_semaphore()
    for d in range(1, nr):
        pl.semaphore_signal(barrier, inc=1, device_id=(lax.rem(r + d, nr), c), device_id_type=MESH)
    for d in range(1, nc):
        pl.semaphore_signal(barrier, inc=1, device_id=(r, lax.rem(c + d, nc)), device_id_type=MESH)

    lane = lax.broadcasted_iota(jnp.int32, (128, 128), 1)

    def prepare(k):
        rows = slice(k * 128, (k + 1) * 128)
        for ref, pot, cat, scale, first, order in (
            (x_ref, f_ref, xc, 2.0 * LOG2E, 0, (0, 1, 0)),
            (y_ref, g_ref, yc, 1.0, 3, (0, 0, 1)),
        ):
            tile = ref[rows, :]
            parts = split(tile * scale)
            for slot, which in enumerate(order):
                cat[rows, slot * D:(slot + 1) * D] = parts[which]
            norm = jnp.sum(tile * tile, axis=1, keepdims=True)
            offset = LOG2E * (2.0 * column(pot[k:k + 1, :]) - norm)
            one = offset.astype(BF16).astype(F32)
            two = (offset - one).astype(BF16).astype(F32)
            three = offset - one - two
            extra = jnp.where(lane < 6, 1.0, 0.0)
            for place, piece in enumerate((one, two, three)):
                extra = jnp.where(lane == first + place, piece, extra)
            cat[rows, 3 * D:] = extra.astype(BF16)

    for k in range(groups):
        prepare(k)

    def soften(left, right, out, peak_slot, round_slot, along_row):
        tall = 256 if size % 256 == 0 else 128
        tops = []
        for k in range(chunks + 1):
            top = jnp.full((8, lane_chunk), -jnp.inf, F32)
            total = jnp.zeros((8, lane_chunk), F32)
            ahead = slice(k * lane_chunk, (k + 1) * lane_chunk)
            lanes = slice((k - 1) * lane_chunk, k * lane_chunk)
            for q in range(size // tall):
                rows = slice(q * tall, (q + 1) * tall)
                if k < chunks:
                    tile = mm(left[rows, :], right[ahead, :], NT)
                    out[rows, ahead] = tile
                    top = jnp.maximum(top, jnp.max(tile.reshape(tall // 8, 8, lane_chunk), axis=0))
                if k:
                    tile = jnp.exp2(out[rows, lanes] - tops[k - 1])
                    out[rows, lanes] = tile
                    total = total + jnp.sum(tile.reshape(tall // 8, 8, lane_chunk), axis=0)
            if k < chunks:
                tops.append(jnp.max(top, axis=0, keepdims=True))
            if k:
                total = jnp.sum(total, axis=0, keepdims=True)
                local = tops[k - 1] + LOG2E * jnp.log(total)
                for w in range(wide):
                    group, part = (k - 1) * wide + w, slice(w * 128, (w + 1) * 128)
                    peak[peak_slot, group:group + 1, :] = tops[k - 1][:, part]
                    send[round_slot, group:group + 1, :] = local[:, part]
                    if (group + 1) % per == 0:
                        if group + 1 == per and not along_row:
                            pl.semaphore_wait(barrier, nr + nc - 2)
                        exchange(round_slot, along_row, group + 1 - per)

    def ring(n):
        return lambda d: min(d % n, -d % n)

    def exchange(slot, along_row, first):
        n = nr if along_row else nc
        hops = (lambda d: ring(nr // cb)(d // cb) + ring(cb)(d % cb)) if along_row else ring(n)
        for d in sorted(range(1, n), key=lambda d: -hops(d)):
            if along_row:
                device = (lax.rem(r // cb + d // cb, nr // cb) * cb + lax.rem(r + d % cb, cb), c)
            else:
                device = (r, lax.rem(c + d, nc))
            pltpu.make_async_remote_copy(
                send.at[slot, pl.ds(first, per)], recv.at[slot, d - 1, pl.ds(first, per)],
                ssem.at[slot], rsem.at[slot], device_id=device, device_id_type=MESH,
            ).start()

    def wait_bytes(ref, sem):
        pltpu.make_async_copy(ref, ref, sem).wait()

    def arrived(slot, n):
        wait_bytes(recv.at[slot, pl.ds(0, n - 1)], rsem.at[slot])

    def total_of(slot, n):
        total = send[slot]
        for d in range(n - 1):
            total = total + recv[slot, d]
        return total

    def norm_scale(slot, n, peak_slot):
        top = send[slot]
        for d in range(n - 1):
            top = jnp.maximum(top, recv[slot, d])
        total = jnp.exp2(send[slot] - top)
        for d in range(n - 1):
            total = total + jnp.exp2(recv[slot, d] - top)
        return jnp.exp2(peak[peak_slot] - top - LOG2E * jnp.log(total))

    def push(matrix, slot, along_row):
        for k in range(groups):
            rows = slice(k * 128, (k + 1) * 128)
            acc = matrix[rows, 0:128] * coef[0:1, :]
            for q in range(1, groups):
                acc = acc + matrix[rows, q * 128:(q + 1) * 128] * coef[q:q + 1, :]
            send[slot, k:k + 1, :] = jnp.sum(acc.T, axis=0, keepdims=True)
            if (k + 1) % per == 0:
                exchange(slot, along_row, k + 1 - per)

    def halves(matrix, high, low):
        def one(k, _):
            rows = pl.ds(pl.multiple_of(k * 32, 32), 32)
            high[rows, :], low[rows, :] = split(matrix[rows, :])
            return 0

        lax.fori_loop(0, size // 32, one, 0)

    def turned(ref, out, out2):
        for k in range(groups):
            lanes = slice(k * 128, (k + 1) * 128)
            tile = ref[lanes, :].T
            out[:, lanes] = tile
            out2[0:D, lanes], out2[D:2 * D, lanes] = split(tile)

    def early(points2, high, low, scale, out):
        for k in range(chunks):
            lanes = slice(k * lane_chunk, (k + 1) * lane_chunk)
            both = mm(points2[...], high[:, lanes], NN)
            tile = both[0:D] + both[D:2 * D] + mm(points2[0:D, :], low[:, lanes], NN)
            for w in range(wide):
                group = k * wide + w
                block = tile[:, w * 128:(w + 1) * 128] * scale[group:group + 1, :]
                out[group * 128:(group + 1) * 128, :] = block.T

    def fill_column(slot, rows_of):
        for k in range(groups):
            cols[slot, k * 128:(k + 1) * 128, :] = column(rows_of[k:k + 1, :])

    def scale_points(points):
        for k in range(groups):
            lanes = slice(k * 128, (k + 1) * 128)
            scaled[0:D, lanes], scaled[D:2 * D, lanes] = split(points[:, lanes] * coef[k:k + 1, :])

    nz = nc // 2
    z_late = [nz // 2, 1] + [e for d in range(nz // 2 - 1, 1, -1) for e in (d, nz - d)] + [nz - 1, 0]
    z_early = sorted(range(nz), key=lambda d: (2 if d == 0 else 1 - d % 2, -min(d, nz - d)))
    ch_r = nr // cb
    r_list = [(o, t) for o in sorted(range(ch_r), key=lambda o: -min(o, ch_r - o)) for t in reversed(range(cb))]

    def z_dest(d):
        return lax.rem(z + d, nz)

    def r_dest(o, t):
        return lax.rem(r // cb + o, ch_r) * cb + lax.rem(r + t, cb)

    def block(index, rows):
        return pl.ds(pl.multiple_of(index * rows, 8), rows)

    def to_partner(source, pair, slot, d, s_sem, r_sem):
        pltpu.make_async_remote_copy(
            source.at[block(z_dest(d) * 2 + 1 - h, sub_c)], pair.at[slot], s_sem, r_sem,
            device_id=(r, z * 2 + 1 - h), device_id_type=MESH,
        ).start()

    def along_z(out, inbox, slot, d, s_sem, r_sem):
        pltpu.make_async_remote_copy(
            out.at[slot], inbox.at[slot], s_sem, r_sem,
            device_id=(r, z_dest(d) * 2 + h), device_id_type=MESH,
        ).start()

    def along_r(source, inbox, slot, o, t, s_sem, r_sem):
        pltpu.make_async_remote_copy(
            source.at[block(r_dest(o, t), sub_r)], inbox.at[slot], s_sem, r_sem,
            device_id=(r_dest(o, t), c), device_id_type=MESH,
        ).start()

    soften(yc, xc, rt, 0, 0, False)
    soften(xc, yc, s, 1, 1, True)
    turned(y_ref, yt, yt2)
    turned(x_ref, xt, xt2)
    arrived(0, nc)
    rho = norm_scale(0, nc, 0)

    coef[...] = rho * sc_ref[...]
    push(rt, 2, True)
    halves(rt, rt_hi, rt_lo)
    early(yt2, rt_hi, rt_lo, rho, ry)
    for slot, d in enumerate(z_early):
        to_partner(ry, ry_pair, slot, d, bulk_s.at[0], bulk_r.at[0])
    arrived(1, nr)
    sigma = norm_scale(1, nr, 1)
    arrived(2, nr)
    target_adj = tc_ref[...] - total_of(2, nr)

    coef[...] = sigma * target_adj
    push(s, 3, False)
    halves(s, s_hi, s_lo)
    wait_bytes(ry_pair, bulk_r.at[0])
    for slot, d in enumerate(z_early):
        ry_send[slot] = ry[block(z_dest(d) * 2 + h, sub_c), :] + ry_pair[slot]
    arrived(3, nc)
    source_adj = sc_ref[...] - total_of(3, nc)

    coef[...] = rho * source_adj
    push(rt, 4, True)
    cut = nz // 2
    for slot in range(cut):
        along_z(ry_send, ry_recv, slot, z_early[slot], bulk_s.at[1], bulk_r.at[1])
    early(xt2, s_hi, s_lo, sigma, sx)
    arrived(4, nr)
    target_adj = tc_ref[...] - total_of(4, nr)

    coef[...] = sigma * target_adj
    push(s, 5, False)
    fill_column(0, sc_ref)
    arrived(5, nc)
    source_adj = sc_ref[...] - total_of(5, nc)

    coef[...] = rho * source_adj
    push(rt, 6, True)
    for slot in range(cut, nz - 1):
        along_z(ry_send, ry_recv, slot, z_early[slot], bulk_s.at[2], bulk_r.at[2])
    arrived(6, nr)
    target_adj = tc_ref[...] - total_of(6, nr)

    coef[...] = sigma * target_adj
    push(s, 7, False)
    scale_points(yt)

    def z_forward(n):
        wait_bytes(zp_pair.at[pl.ds(2 * n, 2)], late_r.at[n])
        for slot in (2 * n, 2 * n + 1):
            zp_send[slot] = zp[block(z_dest(z_late[slot]) * 2 + h, sub_c), :] + zp_pair[slot]
            if slot < nz - 1:
                along_z(zp_send, zp_recv, slot, z_late[slot], late_s.at[nz // 2], late_r.at[nz // 2])

    for n in range(nz // 2):
        pair = [block(z_dest(z_late[slot]), 2 * sub_c) for slot in (2 * n, 2 * n + 1)]
        both = mm(jnp.concatenate([s_hi[rows, :] for rows in pair]), scaled[...], NT)
        moved = both[:, 0:D] + both[:, D:2 * D]
        moved = moved + mm(jnp.concatenate([s_lo[rows, :] for rows in pair]), scaled[0:D, :], NT)
        for place, rows in enumerate(pair):
            zp[rows, :] = moved[2 * sub_c * place:2 * sub_c * (place + 1)]
        for slot in (2 * n, 2 * n + 1):
            to_partner(zp, zp_pair, slot, z_late[slot], late_s.at[n], late_r.at[n])
        if n:
            z_forward(n - 1)
    z_forward(nz // 2 - 1)
    fill_column(2, target_adj)
    sx[...] = sx[...] * cols[2]

    arrived(7, nc)
    source_adj = sc_ref[...] - total_of(7, nc)

    coef[...] = rho * source_adj
    scale_points(xt)
    tall_r = cb * sub_r
    for n in range(ch_r):
        rows = block(lax.rem(r // cb + r_list[n * cb][0], ch_r), tall_r)
        both = mm(rt_hi[rows, :], scaled[...], NT)
        moved = both[:, 0:D] + both[:, D:2 * D] + mm(rt_lo[rows, :], scaled[0:D, :], NT)
        acc = rt[rows, 0:128] * coef[0:1, :]
        for q in range(1, groups):
            acc = acc + rt[rows, q * 128:(q + 1) * 128] * coef[q:q + 1, :]
        tp[rows, :] = y_ref[rows, :] * jnp.sum(acc, axis=1, keepdims=True) - moved - sx[rows, :]
        for slot in range(n * cb, (n + 1) * cb):
            if slot < nr - 1:
                along_r(tp, tp_recv, slot, *r_list[slot], late_s.at[nz // 2 + 1], late_r.at[nz // 2 + 1])

    fill_column(1, source_adj)
    own_c, own_r = block(c, sub_c), block(r, sub_r)
    wait_bytes(ry_recv.at[pl.ds(0, cut)], bulk_r.at[1])
    wait_bytes(ry_recv.at[pl.ds(cut, nz - 1 - cut)], bulk_r.at[2])
    moved = ry_send[nz - 1]
    for slot in range(nz - 1):
        moved = moved + ry_recv[slot]
    wait_bytes(zp_recv, late_r.at[nz // 2])
    late = zp_send[nz - 1]
    for slot in range(nz - 1):
        late = late + zp_recv[slot]
    out_ref[0:sub_c, :] = x_ref[own_c, :] * cols[0, own_c, :] - cols[1, own_c, :] * moved - late
    wait_bytes(tp_recv, late_r.at[nz // 2 + 1])
    late = tp[own_r, :]
    for slot in range(nr - 1):
        late = late + tp_recv[slot]
    out_ref[sub_c:sub_c + sub_r, :] = cols[2, own_r, :] * y_ref[own_r, :] + late

    for slot, n in enumerate((nc, nr, nr, nc, nr, nc, nr, nc)):
        wait_bytes(recv.at[slot, pl.ds(0, n - 1)], ssem.at[slot])
    wait_bytes(ry_pair, bulk_s.at[0])
    wait_bytes(ry_recv.at[pl.ds(0, cut)], bulk_s.at[1])
    wait_bytes(ry_recv.at[pl.ds(cut, nz - 1 - cut)], bulk_s.at[2])
    for n in range(nz // 2):
        wait_bytes(zp_pair.at[pl.ds(2 * n, 2)], late_s.at[n])
    wait_bytes(zp_recv, late_s.at[nz // 2])
    wait_bytes(tp_recv, late_s.at[nz // 2 + 1])


def shards(nr, nc, cb, lane_chunk, pieces, x, y, f, g, sc, tc):
    size = x.shape[0]
    groups = size // 128
    sub_r, sub_c = size // nr, size // nc
    vectors = [v.reshape(groups, 128) for v in (f, g, sc, tc)]
    vmem = pl.BlockSpec(memory_space=pltpu.VMEM)
    peers = max(nr, nc) - 1
    nz = nc // 2
    square = (size, size)
    both = pl.pallas_call(
        functools.partial(kernel, nr, nc, cb, lane_chunk, pieces),
        out_shape=jax.ShapeDtypeStruct((sub_c + sub_r, D), F32),
        in_specs=[vmem] * 6,
        out_specs=vmem,
        scratch_shapes=[
            pltpu.VMEM((size, 4 * D), BF16),
            pltpu.VMEM((size, 4 * D), BF16),
            pltpu.VMEM(square, F32),
            pltpu.VMEM(square, F32),
            pltpu.VMEM(square, BF16),
            pltpu.VMEM(square, BF16),
            pltpu.VMEM(square, BF16),
            pltpu.VMEM(square, BF16),
            pltpu.VMEM((D, size), F32),
            pltpu.VMEM((D, size), F32),
            pltpu.VMEM((2 * D, size), BF16),
            pltpu.VMEM((2 * D, size), BF16),
            pltpu.VMEM((2 * D, size), BF16),
            pltpu.VMEM((2, groups, 128), F32),
            pltpu.VMEM((groups, 128), F32),
            pltpu.VMEM((8, groups, 128), F32),
            pltpu.VMEM((8, peers, groups, 128), F32),
            pltpu.SemaphoreType.DMA((8,)),
            pltpu.SemaphoreType.DMA((8,)),
            pltpu.VMEM((size, D), F32),
            pltpu.VMEM((nz, sub_c, D), F32),
            pltpu.VMEM((nz, sub_c, D), F32),
            pltpu.VMEM((nz - 1, sub_c, D), F32),
            pltpu.VMEM((size, D), F32),
            pltpu.VMEM((size, D), F32),
            pltpu.VMEM((nz, sub_c, D), F32),
            pltpu.VMEM((nz, sub_c, D), F32),
            pltpu.VMEM((nz - 1, sub_c, D), F32),
            pltpu.VMEM((size, D), F32),
            pltpu.VMEM((nr - 1, sub_r, D), F32),
            pltpu.VMEM((3, size, D), F32),
            pltpu.SemaphoreType.DMA((3,)),
            pltpu.SemaphoreType.DMA((3,)),
            pltpu.SemaphoreType.DMA((nz // 2 + 2,)),
            pltpu.SemaphoreType.DMA((nz // 2 + 2,)),
        ],
        compiler_params=pltpu.CompilerParams(
            collective_id=0, has_side_effects=True, vmem_limit_bytes=62 << 20
        ),
    )(x, y, *vectors)
    return both[:sub_c], both[sub_c:]


def solution(mesh, cb=4, lane_chunk=256, pieces=1):
    in_specs = (P("row", None), P("col", None), P("row"), P("col"), P("row"), P("col"))
    out_specs = (P(("row", "col"), None), P(("col", "row"), None))
    body = functools.partial(shards, mesh.shape["row"], mesh.shape["col"], cb, lane_chunk, pieces)
    return jax.shard_map(body, mesh=mesh, in_specs=in_specs, out_specs=out_specs, check_vma=False)
```

```python
import functools

import jax
import jax.numpy as jnp
from jax import lax
from jax.experimental import pallas as pl
from jax.experimental.pallas import tpu as pltpu
from jax.sharding import PartitionSpec as P

MESH = pl.DeviceIdType.MESH
F32 = jnp.float32
BF16 = jnp.bfloat16
LOG2E = 1.4426950408889634
D = 128
NT = (((1,), (1,)), ((), ()))
NN = (((1,), (0,)), ((), ()))


def mm(left, right, dims):
    return lax.dot_general(left, right, dims, preferred_element_type=F32)


def split(value):
    high = value.astype(BF16)
    return high, (value - high.astype(F32)).astype(BF16)


def column(row):
    return jnp.broadcast_to(row, (128, 128)).T


def kernel(
    nr, nc, cb, lane_chunk, pieces,
    x_ref, y_ref, f_ref, g_ref, sc_ref, tc_ref, out_ref,
    xc, yc, rt, s, rt_hi, rt_lo, s_hi, s_lo, xt, yt, xt2, yt2, scaled,
    peak, coef, send, recv, ssem, rsem,
    ry, ry_pair, ry_send, ry_recv, sx,
    zp, zp_pair, zp_send, zp_recv, tp, tp_recv, cols,
    bulk_s, bulk_r, late_s, late_r,
):
    size = x_ref.shape[0]
    groups = size // 128
    chunks = size // lane_chunk
    wide = lane_chunk // 128
    per = groups // pieces
    sub_r, sub_c = size // nr, size // nc
    r, c = lax.axis_index("row"), lax.axis_index("col")
    z, h = c // 2, lax.rem(c, 2)

    barrier = pltpu.get_barrier_semaphore()
    for d in range(1, nr):
        pl.semaphore_signal(barrier, inc=1, device_id=(lax.rem(r + d, nr), c), device_id_type=MESH)
    for d in range(1, nc):
        pl.semaphore_signal(barrier, inc=1, device_id=(r, lax.rem(c + d, nc)), device_id_type=MESH)

    lane = lax.broadcasted_iota(jnp.int32, (128, 128), 1)

    def prepare(k):
        rows = slice(k * 128, (k + 1) * 128)
        for ref, pot, cat, scale, first, order in (
            (x_ref, f_ref, xc, 2.0 * LOG2E, 0, (0, 1, 0)),
            (y_ref, g_ref, yc, 1.0, 3, (0, 0, 1)),
        ):
            tile = ref[rows, :]
            parts = split(tile * scale)
            for slot, which in enumerate(order):
                cat[rows, slot * D:(slot + 1) * D] = parts[which]
            norm = jnp.sum(tile * tile, axis=1, keepdims=True)
            offset = LOG2E * (2.0 * column(pot[k:k + 1, :]) - norm)
            one = offset.astype(BF16).astype(F32)
            two = (offset - one).astype(BF16).astype(F32)
            three = offset - one - two
            extra = jnp.where(lane < 6, 1.0, 0.0)
            for place, piece in enumerate((one, two, three)):
                extra = jnp.where(lane == first + place, piece, extra)
            cat[rows, 3 * D:] = extra.astype(BF16)

    for k in range(groups):
        prepare(k)

    def soften(left, right, out, peak_slot, round_slot, along_row):
        tall = 256 if size % 256 == 0 else 128
        tops = []
        for k in range(chunks + 1):
            top = jnp.full((8, lane_chunk), -jnp.inf, F32)
            total = jnp.zeros((8, lane_chunk), F32)
            ahead = slice(k * lane_chunk, (k + 1) * lane_chunk)
            lanes = slice((k - 1) * lane_chunk, k * lane_chunk)
            for q in range(size // tall):
                rows = slice(q * tall, (q + 1) * tall)
                if k < chunks:
                    tile = mm(left[rows, :], right[ahead, :], NT)
                    out[rows, ahead] = tile
                    top = jnp.maximum(top, jnp.max(tile.reshape(tall // 8, 8, lane_chunk), axis=0))
                if k:
                    tile = jnp.exp2(out[rows, lanes] - tops[k - 1])
                    out[rows, lanes] = tile
                    total = total + jnp.sum(tile.reshape(tall // 8, 8, lane_chunk), axis=0)
            if k < chunks:
                tops.append(jnp.max(top, axis=0, keepdims=True))
            if k:
                total = jnp.sum(total, axis=0, keepdims=True)
                local = tops[k - 1] + LOG2E * jnp.log(total)
                for w in range(wide):
                    group, part = (k - 1) * wide + w, slice(w * 128, (w + 1) * 128)
                    peak[peak_slot, group:group + 1, :] = tops[k - 1][:, part]
                    send[round_slot, group:group + 1, :] = local[:, part]
                    if (group + 1) % per == 0:
                        if group + 1 == per and not along_row:
                            pl.semaphore_wait(barrier, nr + nc - 2)
                        exchange(round_slot, along_row, group + 1 - per)

    def ring(n):
        return lambda d: min(d % n, -d % n)

    def exchange(slot, along_row, first):
        n = nr if along_row else nc
        hops = (lambda d: ring(nr // cb)(d // cb) + ring(cb)(d % cb)) if along_row else ring(n)
        for d in sorted(range(1, n), key=lambda d: -hops(d)):
            if along_row:
                device = (lax.rem(r // cb + d // cb, nr // cb) * cb + lax.rem(r + d % cb, cb), c)
            else:
                device = (r, lax.rem(c + d, nc))
            pltpu.make_async_remote_copy(
                send.at[slot, pl.ds(first, per)], recv.at[slot, d - 1, pl.ds(first, per)],
                ssem.at[slot], rsem.at[slot], device_id=device, device_id_type=MESH,
            ).start()

    def wait_bytes(ref, sem):
        pltpu.make_async_copy(ref, ref, sem).wait()

    def arrived(slot, n):
        wait_bytes(recv.at[slot, pl.ds(0, n - 1)], rsem.at[slot])

    def total_of(slot, n):
        total = send[slot]
        for d in range(n - 1):
            total = total + recv[slot, d]
        return total

    def norm_scale(slot, n, peak_slot):
        top = send[slot]
        for d in range(n - 1):
            top = jnp.maximum(top, recv[slot, d])
        total = jnp.exp2(send[slot] - top)
        for d in range(n - 1):
            total = total + jnp.exp2(recv[slot, d] - top)
        return jnp.exp2(peak[peak_slot] - top - LOG2E * jnp.log(total))

    def push(matrix, slot, along_row):
        for k in range(groups):
            rows = slice(k * 128, (k + 1) * 128)
            acc = matrix[rows, 0:128] * coef[0:1, :]
            for q in range(1, groups):
                acc = acc + matrix[rows, q * 128:(q + 1) * 128] * coef[q:q + 1, :]
            send[slot, k:k + 1, :] = jnp.sum(acc.T, axis=0, keepdims=True)
            if (k + 1) % per == 0:
                exchange(slot, along_row, k + 1 - per)

    def halves(matrix, high, low):
        def one(k, _):
            rows = pl.ds(pl.multiple_of(k * 32, 32), 32)
            high[rows, :], low[rows, :] = split(matrix[rows, :])
            return 0

        lax.fori_loop(0, size // 32, one, 0)

    def turned(ref, out, out2):
        for k in range(groups):
            lanes = slice(k * 128, (k + 1) * 128)
            tile = ref[lanes, :].T
            out[:, lanes] = tile
            out2[0:D, lanes], out2[D:2 * D, lanes] = split(tile)

    def early(points2, high, low, scale, out):
        for k in range(chunks):
            lanes = slice(k * lane_chunk, (k + 1) * lane_chunk)
            both = mm(points2[...], high[:, lanes], NN)
            tile = both[0:D] + both[D:2 * D] + mm(points2[0:D, :], low[:, lanes], NN)
            for w in range(wide):
                group = k * wide + w
                block = tile[:, w * 128:(w + 1) * 128] * scale[group:group + 1, :]
                out[group * 128:(group + 1) * 128, :] = block.T

    def fill_column(slot, rows_of):
        for k in range(groups):
            cols[slot, k * 128:(k + 1) * 128, :] = column(rows_of[k:k + 1, :])

    def scale_points(points):
        for k in range(groups):
            lanes = slice(k * 128, (k + 1) * 128)
            scaled[0:D, lanes], scaled[D:2 * D, lanes] = split(points[:, lanes] * coef[k:k + 1, :])

    nz = nc // 2
    z_late = [nz // 2, 1] + [e for d in range(nz // 2 - 1, 1, -1) for e in (d, nz - d)] + [nz - 1, 0]
    z_early = sorted(range(nz), key=lambda d: (2 if d == 0 else 1 - d % 2, -min(d, nz - d)))
    ch_r = nr // cb
    r_list = [(o, t) for o in sorted(range(ch_r), key=lambda o: -min(o, ch_r - o)) for t in reversed(range(cb))]

    def z_dest(d):
        return lax.rem(z + d, nz)

    def r_dest(o, t):
        return lax.rem(r // cb + o, ch_r) * cb + lax.rem(r + t, cb)

    def block(index, rows):
        return pl.ds(pl.multiple_of(index * rows, 8), rows)

    def to_partner(source, pair, slot, d, s_sem, r_sem):
        pltpu.make_async_remote_copy(
            source.at[block(z_dest(d) * 2 + 1 - h, sub_c)], pair.at[slot], s_sem, r_sem,
            device_id=(r, z * 2 + 1 - h), device_id_type=MESH,
        ).start()

    def along_z(out, inbox, slot, d, s_sem, r_sem):
        pltpu.make_async_remote_copy(
            out.at[slot], inbox.at[slot], s_sem, r_sem,
            device_id=(r, z_dest(d) * 2 + h), device_id_type=MESH,
        ).start()

    def along_r(source, inbox, slot, o, t, s_sem, r_sem):
        pltpu.make_async_remote_copy(
            source.at[block(r_dest(o, t), sub_r)], inbox.at[slot], s_sem, r_sem,
            device_id=(r_dest(o, t), c), device_id_type=MESH,
        ).start()

    soften(yc, xc, rt, 0, 0, False)
    soften(xc, yc, s, 1, 1, True)
    turned(y_ref, yt, yt2)
    turned(x_ref, xt, xt2)
    arrived(0, nc)
    rho = norm_scale(0, nc, 0)

    coef[...] = rho * sc_ref[...]
    push(rt, 2, True)
    halves(rt, rt_hi, rt_lo)
    early(yt2, rt_hi, rt_lo, rho, ry)
    for slot, d in enumerate(z_early):
        to_partner(ry, ry_pair, slot, d, bulk_s.at[0], bulk_r.at[0])
    arrived(1, nr)
    sigma = norm_scale(1, nr, 1)
    arrived(2, nr)
    target_adj = tc_ref[...] - total_of(2, nr)

    coef[...] = sigma * target_adj
    push(s, 3, False)
    halves(s, s_hi, s_lo)
    wait_bytes(ry_pair, bulk_r.at[0])
    for slot, d in enumerate(z_early):
        ry_send[slot] = ry[block(z_dest(d) * 2 + h, sub_c), :] + ry_pair[slot]
    arrived(3, nc)
    source_adj = sc_ref[...] - total_of(3, nc)

    coef[...] = rho * source_adj
    push(rt, 4, True)
    cut = nz // 2
    for slot in range(cut):
        along_z(ry_send, ry_recv, slot, z_early[slot], bulk_s.at[1], bulk_r.at[1])
    early(xt2, s_hi, s_lo, sigma, sx)
    arrived(4, nr)
    target_adj = tc_ref[...] - total_of(4, nr)

    coef[...] = sigma * target_adj
    push(s, 5, False)
    fill_column(0, sc_ref)
    arrived(5, nc)
    source_adj = sc_ref[...] - total_of(5, nc)

    coef[...] = rho * source_adj
    push(rt, 6, True)
    for slot in range(cut, nz - 1):
        along_z(ry_send, ry_recv, slot, z_early[slot], bulk_s.at[2], bulk_r.at[2])
    arrived(6, nr)
    target_adj = tc_ref[...] - total_of(6, nr)

    coef[...] = sigma * target_adj
    push(s, 7, False)
    scale_points(yt)

    def z_forward(n):
        wait_bytes(zp_pair.at[pl.ds(2 * n, 2)], late_r.at[n])
        for slot in (2 * n, 2 * n + 1):
            zp_send[slot] = zp[block(z_dest(z_late[slot]) * 2 + h, sub_c), :] + zp_pair[slot]
            if slot < nz - 1:
                along_z(zp_send, zp_recv, slot, z_late[slot], late_s.at[nz // 2], late_r.at[nz // 2])

    for n in range(nz // 2):
        pair = [block(z_dest(z_late[slot]), 2 * sub_c) for slot in (2 * n, 2 * n + 1)]
        both = mm(jnp.concatenate([s_hi[rows, :] for rows in pair]), scaled[...], NT)
        moved = both[:, 0:D] + both[:, D:2 * D]
        moved = moved + mm(jnp.concatenate([s_lo[rows, :] for rows in pair]), scaled[0:D, :], NT)
        for place, rows in enumerate(pair):
            zp[rows, :] = moved[2 * sub_c * place:2 * sub_c * (place + 1)]
        for slot in (2 * n, 2 * n + 1):
            to_partner(zp, zp_pair, slot, z_late[slot], late_s.at[n], late_r.at[n])
        if n > 1:
            z_forward(n - 2)
    fill_column(2, target_adj)
    sx[...] = sx[...] * cols[2]
    z_forward(nz // 2 - 2)

    arrived(7, nc)
    source_adj = sc_ref[...] - total_of(7, nc)

    coef[...] = rho * source_adj
    scale_points(xt)
    tall_r = cb * sub_r
    for n in range(ch_r):
        rows = block(lax.rem(r // cb + r_list[n * cb][0], ch_r), tall_r)
        both = mm(rt_hi[rows, :], scaled[...], NT)
        moved = both[:, 0:D] + both[:, D:2 * D] + mm(rt_lo[rows, :], scaled[0:D, :], NT)
        acc = rt[rows, 0:128] * coef[0:1, :]
        for q in range(1, groups):
            acc = acc + rt[rows, q * 128:(q + 1) * 128] * coef[q:q + 1, :]
        tp[rows, :] = y_ref[rows, :] * jnp.sum(acc, axis=1, keepdims=True) - moved - sx[rows, :]
        for slot in range(n * cb, (n + 1) * cb):
            if slot < nr - 1:
                along_r(tp, tp_recv, slot, *r_list[slot], late_s.at[nz // 2 + 1], late_r.at[nz // 2 + 1])
        if n == 0:
            z_forward(nz // 2 - 1)

    fill_column(1, source_adj)
    own_c, own_r = block(c, sub_c), block(r, sub_r)
    wait_bytes(ry_recv.at[pl.ds(0, cut)], bulk_r.at[1])
    wait_bytes(ry_recv.at[pl.ds(cut, nz - 1 - cut)], bulk_r.at[2])
    moved = ry_send[nz - 1]
    for slot in range(nz - 1):
        moved = moved + ry_recv[slot]
    wait_bytes(zp_recv, late_r.at[nz // 2])
    late = zp_send[nz - 1]
    for slot in range(nz - 1):
        late = late + zp_recv[slot]
    out_ref[0:sub_c, :] = x_ref[own_c, :] * cols[0, own_c, :] - cols[1, own_c, :] * moved - late
    wait_bytes(tp_recv, late_r.at[nz // 2 + 1])
    late = tp[own_r, :]
    for slot in range(nr - 1):
        late = late + tp_recv[slot]
    out_ref[sub_c:sub_c + sub_r, :] = cols[2, own_r, :] * y_ref[own_r, :] + late

    for slot, n in enumerate((nc, nr, nr, nc, nr, nc, nr, nc)):
        wait_bytes(recv.at[slot, pl.ds(0, n - 1)], ssem.at[slot])
    wait_bytes(ry_pair, bulk_s.at[0])
    wait_bytes(ry_recv.at[pl.ds(0, cut)], bulk_s.at[1])
    wait_bytes(ry_recv.at[pl.ds(cut, nz - 1 - cut)], bulk_s.at[2])
    for n in range(nz // 2):
        wait_bytes(zp_pair.at[pl.ds(2 * n, 2)], late_s.at[n])
    wait_bytes(zp_recv, late_s.at[nz // 2])
    wait_bytes(tp_recv, late_s.at[nz // 2 + 1])


def shards(nr, nc, cb, lane_chunk, pieces, x, y, f, g, sc, tc):
    size = x.shape[0]
    groups = size // 128
    sub_r, sub_c = size // nr, size // nc
    vectors = [v.reshape(groups, 128) for v in (f, g, sc, tc)]
    vmem = pl.BlockSpec(memory_space=pltpu.VMEM)
    peers = max(nr, nc) - 1
    nz = nc // 2
    square = (size, size)
    both = pl.pallas_call(
        functools.partial(kernel, nr, nc, cb, lane_chunk, pieces),
        out_shape=jax.ShapeDtypeStruct((sub_c + sub_r, D), F32),
        in_specs=[vmem] * 6,
        out_specs=vmem,
        scratch_shapes=[
            pltpu.VMEM((size, 4 * D), BF16),
            pltpu.VMEM((size, 4 * D), BF16),
            pltpu.VMEM(square, F32),
            pltpu.VMEM(square, F32),
            pltpu.VMEM(square, BF16),
            pltpu.VMEM(square, BF16),
            pltpu.VMEM(square, BF16),
            pltpu.VMEM(square, BF16),
            pltpu.VMEM((D, size), F32),
            pltpu.VMEM((D, size), F32),
            pltpu.VMEM((2 * D, size), BF16),
            pltpu.VMEM((2 * D, size), BF16),
            pltpu.VMEM((2 * D, size), BF16),
            pltpu.VMEM((2, groups, 128), F32),
            pltpu.VMEM((groups, 128), F32),
            pltpu.VMEM((8, groups, 128), F32),
            pltpu.VMEM((8, peers, groups, 128), F32),
            pltpu.SemaphoreType.DMA((8,)),
            pltpu.SemaphoreType.DMA((8,)),
            pltpu.VMEM((size, D), F32),
            pltpu.VMEM((nz, sub_c, D), F32),
            pltpu.VMEM((nz, sub_c, D), F32),
            pltpu.VMEM((nz - 1, sub_c, D), F32),
            pltpu.VMEM((size, D), F32),
            pltpu.VMEM((size, D), F32),
            pltpu.VMEM((nz, sub_c, D), F32),
            pltpu.VMEM((nz, sub_c, D), F32),
            pltpu.VMEM((nz - 1, sub_c, D), F32),
            pltpu.VMEM((size, D), F32),
            pltpu.VMEM((nr - 1, sub_r, D), F32),
            pltpu.VMEM((3, size, D), F32),
            pltpu.SemaphoreType.DMA((3,)),
            pltpu.SemaphoreType.DMA((3,)),
            pltpu.SemaphoreType.DMA((nz // 2 + 2,)),
            pltpu.SemaphoreType.DMA((nz // 2 + 2,)),
        ],
        compiler_params=pltpu.CompilerParams(
            collective_id=0, has_side_effects=True, vmem_limit_bytes=62 << 20
        ),
    )(x, y, *vectors)
    return both[:sub_c], both[sub_c:]


def solution(mesh, cb=4, lane_chunk=256, pieces=1):
    in_specs = (P("row", None), P("col", None), P("row"), P("col"), P("row"), P("col"))
    out_specs = (P(("row", "col"), None), P(("col", "row"), None))
    body = functools.partial(shards, mesh.shape["row"], mesh.shape["col"], cb, lane_chunk, pieces)
    return jax.shard_map(body, mesh=mesh, in_specs=in_specs, out_specs=out_specs, check_vma=False)
```

```python
import functools

import jax
import jax.numpy as jnp
from jax import lax
from jax.experimental import pallas as pl
from jax.experimental.pallas import tpu as pltpu
from jax.sharding import PartitionSpec as P

MESH = pl.DeviceIdType.MESH
F32 = jnp.float32
BF16 = jnp.bfloat16
LOG2E = 1.4426950408889634
D = 128
NT = (((1,), (1,)), ((), ()))
NN = (((1,), (0,)), ((), ()))


def mm(left, right, dims):
    return lax.dot_general(left, right, dims, preferred_element_type=F32)


def split(value):
    high = value.astype(BF16)
    return high, (value - high.astype(F32)).astype(BF16)


def column(row):
    return jnp.broadcast_to(row, (128, 128)).T


def kernel(
    nr, nc, cb, lane_chunk, pieces,
    x_ref, y_ref, f_ref, g_ref, sc_ref, tc_ref, out_ref,
    xc, yc, rt, s, rt_hi, rt_lo, s_hi, s_lo, xt, yt, xt2, yt2, scaled,
    peak, coef, send, recv, ssem, rsem,
    ry, ry_pair, ry_send, ry_recv, sx,
    zp, zp_pair, zp_send, zp_recv, tp, tp_recv, cols,
    bulk_s, bulk_r, late_s, late_r,
):
    size = x_ref.shape[0]
    groups = size // 128
    chunks = size // lane_chunk
    wide = lane_chunk // 128
    per = groups // pieces
    sub_r, sub_c = size // nr, size // nc
    r, c = lax.axis_index("row"), lax.axis_index("col")
    z, h = c // 2, lax.rem(c, 2)

    barrier = pltpu.get_barrier_semaphore()
    for d in range(1, nr):
        pl.semaphore_signal(barrier, inc=1, device_id=(lax.rem(r + d, nr), c), device_id_type=MESH)
    for d in range(1, nc):
        pl.semaphore_signal(barrier, inc=1, device_id=(r, lax.rem(c + d, nc)), device_id_type=MESH)

    lane = lax.broadcasted_iota(jnp.int32, (128, 128), 1)

    def prepare(k):
        rows = slice(k * 128, (k + 1) * 128)
        for ref, pot, cat, scale, first, order in (
            (x_ref, f_ref, xc, 2.0 * LOG2E, 0, (0, 1, 0)),
            (y_ref, g_ref, yc, 1.0, 3, (0, 0, 1)),
        ):
            tile = ref[rows, :]
            parts = split(tile * scale)
            for slot, which in enumerate(order):
                cat[rows, slot * D:(slot + 1) * D] = parts[which]
            norm = jnp.sum(tile * tile, axis=1, keepdims=True)
            offset = LOG2E * (2.0 * column(pot[k:k + 1, :]) - norm)
            one = offset.astype(BF16).astype(F32)
            two = (offset - one).astype(BF16).astype(F32)
            three = offset - one - two
            extra = jnp.where(lane < 6, 1.0, 0.0)
            for place, piece in enumerate((one, two, three)):
                extra = jnp.where(lane == first + place, piece, extra)
            cat[rows, 3 * D:] = extra.astype(BF16)

    for k in range(groups):
        prepare(k)

    def soften(left, right, out, peak_slot, round_slot, along_row):
        tall = 256 if size % 256 == 0 else 128
        tops = []
        for k in range(chunks + 1):
            top = jnp.full((8, lane_chunk), -jnp.inf, F32)
            total = jnp.zeros((8, lane_chunk), F32)
            ahead = slice(k * lane_chunk, (k + 1) * lane_chunk)
            lanes = slice((k - 1) * lane_chunk, k * lane_chunk)
            for q in range(size // tall):
                rows = slice(q * tall, (q + 1) * tall)
                if k < chunks:
                    tile = mm(left[rows, :], right[ahead, :], NT)
                    out[rows, ahead] = tile
                    top = jnp.maximum(top, jnp.max(tile.reshape(tall // 8, 8, lane_chunk), axis=0))
                if k:
                    tile = jnp.exp2(out[rows, lanes] - tops[k - 1])
                    out[rows, lanes] = tile
                    total = total + jnp.sum(tile.reshape(tall // 8, 8, lane_chunk), axis=0)
            if k < chunks:
                tops.append(jnp.max(top, axis=0, keepdims=True))
            if k:
                total = jnp.sum(total, axis=0, keepdims=True)
                local = tops[k - 1] + LOG2E * jnp.log(total)
                for w in range(wide):
                    group, part = (k - 1) * wide + w, slice(w * 128, (w + 1) * 128)
                    peak[peak_slot, group:group + 1, :] = tops[k - 1][:, part]
                    send[round_slot, group:group + 1, :] = local[:, part]
                    if (group + 1) % per == 0:
                        if group + 1 == per and not along_row:
                            pl.semaphore_wait(barrier, nr + nc - 2)
                        exchange(round_slot, along_row, group + 1 - per)

    def ring(n):
        return lambda d: min(d % n, -d % n)

    def exchange(slot, along_row, first):
        n = nr if along_row else nc
        hops = (lambda d: ring(nr // cb)(d // cb) + ring(cb)(d % cb)) if along_row else ring(n)
        for d in sorted(range(1, n), key=lambda d: -hops(d)):
            if along_row:
                device = (lax.rem(r // cb + d // cb, nr // cb) * cb + lax.rem(r + d % cb, cb), c)
            else:
                device = (r, lax.rem(c + d, nc))
            pltpu.make_async_remote_copy(
                send.at[slot, pl.ds(first, per)], recv.at[slot, d - 1, pl.ds(first, per)],
                ssem.at[slot], rsem.at[slot], device_id=device, device_id_type=MESH,
            ).start()

    def wait_bytes(ref, sem):
        pltpu.make_async_copy(ref, ref, sem).wait()

    def arrived(slot, n):
        wait_bytes(recv.at[slot, pl.ds(0, n - 1)], rsem.at[slot])

    def total_of(slot, n):
        total = send[slot]
        for d in range(n - 1):
            total = total + recv[slot, d]
        return total

    def norm_scale(slot, n, peak_slot):
        top = send[slot]
        for d in range(n - 1):
            top = jnp.maximum(top, recv[slot, d])
        total = jnp.exp2(send[slot] - top)
        for d in range(n - 1):
            total = total + jnp.exp2(recv[slot, d] - top)
        return jnp.exp2(peak[peak_slot] - top - LOG2E * jnp.log(total))

    def push(matrix, slot, along_row):
        for k in range(groups):
            rows = slice(k * 128, (k + 1) * 128)
            acc = matrix[rows, 0:128] * coef[0:1, :]
            for q in range(1, groups):
                acc = acc + matrix[rows, q * 128:(q + 1) * 128] * coef[q:q + 1, :]
            send[slot, k:k + 1, :] = jnp.sum(acc.T, axis=0, keepdims=True)
            if (k + 1) % per == 0:
                exchange(slot, along_row, k + 1 - per)

    def halves(matrix, high, low):
        def one(k, _):
            rows = pl.ds(pl.multiple_of(k * 32, 32), 32)
            high[rows, :], low[rows, :] = split(matrix[rows, :])
            return 0

        lax.fori_loop(0, size // 32, one, 0)

    def turned(ref, out, out2):
        for k in range(groups):
            lanes = slice(k * 128, (k + 1) * 128)
            tile = ref[lanes, :].T
            out[:, lanes] = tile
            out2[0:D, lanes], out2[D:2 * D, lanes] = split(tile)

    def early(points2, high, low, scale, out):
        for k in range(chunks):
            lanes = slice(k * lane_chunk, (k + 1) * lane_chunk)
            both = mm(points2[...], high[:, lanes], NN)
            tile = both[0:D] + both[D:2 * D] + mm(points2[0:D, :], low[:, lanes], NN)
            for w in range(wide):
                group = k * wide + w
                block = tile[:, w * 128:(w + 1) * 128] * scale[group:group + 1, :]
                out[group * 128:(group + 1) * 128, :] = block.T

    def fill_column(slot, rows_of):
        for k in range(groups):
            cols[slot, k * 128:(k + 1) * 128, :] = column(rows_of[k:k + 1, :])

    def scale_points(points, scaled):
        for k in range(groups):
            lanes = slice(k * 128, (k + 1) * 128)
            scaled[0:D, lanes], scaled[D:2 * D, lanes] = split(points[:, lanes] * coef[k:k + 1, :])

    nz = nc // 2
    z_late = [nz // 2, 1] + [e for d in range(nz // 2 - 1, 1, -1) for e in (d, nz - d)] + [nz - 1, 0]
    z_early = sorted(range(nz), key=lambda d: (2 if d == 0 else 1 - d % 2, -min(d, nz - d)))
    ch_r = nr // cb
    r_list = [(o, t) for o in sorted(range(ch_r), key=lambda o: -min(o, ch_r - o)) for t in reversed(range(cb))]

    def z_dest(d):
        return lax.rem(z + d, nz)

    def r_dest(o, t):
        return lax.rem(r // cb + o, ch_r) * cb + lax.rem(r + t, cb)

    def block(index, rows):
        return pl.ds(pl.multiple_of(index * rows, 8), rows)

    def to_partner(source, pair, slot, d, s_sem, r_sem):
        pltpu.make_async_remote_copy(
            source.at[block(z_dest(d) * 2 + 1 - h, sub_c)], pair.at[slot], s_sem, r_sem,
            device_id=(r, z * 2 + 1 - h), device_id_type=MESH,
        ).start()

    def along_z(out, inbox, slot, d, s_sem, r_sem):
        pltpu.make_async_remote_copy(
            out.at[slot], inbox.at[slot], s_sem, r_sem,
            device_id=(r, z_dest(d) * 2 + h), device_id_type=MESH,
        ).start()

    def along_r(source, inbox, slot, o, t, s_sem, r_sem):
        pltpu.make_async_remote_copy(
            source.at[block(r_dest(o, t), sub_r)], inbox.at[slot], s_sem, r_sem,
            device_id=(r_dest(o, t), c), device_id_type=MESH,
        ).start()

    soften(yc, xc, rt, 0, 0, False)
    soften(xc, yc, s, 1, 1, True)
    turned(y_ref, yt, yt2)
    turned(x_ref, xt, xt2)
    arrived(0, nc)
    rho = norm_scale(0, nc, 0)

    coef[...] = rho * sc_ref[...]
    push(rt, 2, True)
    halves(rt, rt_hi, rt_lo)
    early(yt2, rt_hi, rt_lo, rho, ry)
    for slot, d in enumerate(z_early):
        to_partner(ry, ry_pair, slot, d, bulk_s.at[0], bulk_r.at[0])
    arrived(1, nr)
    sigma = norm_scale(1, nr, 1)
    arrived(2, nr)
    target_adj = tc_ref[...] - total_of(2, nr)

    coef[...] = sigma * target_adj
    push(s, 3, False)
    halves(s, s_hi, s_lo)
    wait_bytes(ry_pair, bulk_r.at[0])
    for slot, d in enumerate(z_early):
        ry_send[slot] = ry[block(z_dest(d) * 2 + h, sub_c), :] + ry_pair[slot]
    arrived(3, nc)
    source_adj = sc_ref[...] - total_of(3, nc)

    coef[...] = rho * source_adj
    push(rt, 4, True)
    cut = nz // 2
    for slot in range(cut):
        along_z(ry_send, ry_recv, slot, z_early[slot], bulk_s.at[1], bulk_r.at[1])
    early(xt2, s_hi, s_lo, sigma, sx)
    arrived(4, nr)
    target_adj = tc_ref[...] - total_of(4, nr)

    coef[...] = sigma * target_adj
    push(s, 5, False)
    fill_column(0, sc_ref)
    arrived(5, nc)
    source_adj = sc_ref[...] - total_of(5, nc)

    coef[...] = rho * source_adj
    push(rt, 6, True)
    for slot in range(cut, nz - 1):
        along_z(ry_send, ry_recv, slot, z_early[slot], bulk_s.at[2], bulk_r.at[2])
    arrived(6, nr)
    target_adj = tc_ref[...] - total_of(6, nr)

    coef[...] = sigma * target_adj
    push(s, 7, False)
    scale_points(yt, scaled)

    def z_forward(n):
        wait_bytes(zp_pair.at[pl.ds(2 * n, 2)], late_r.at[n])
        for slot in (2 * n, 2 * n + 1):
            zp_send[slot] = zp[block(z_dest(z_late[slot]) * 2 + h, sub_c), :] + zp_pair[slot]
            if slot < nz - 1:
                along_z(zp_send, zp_recv, slot, z_late[slot], late_s.at[nz // 2], late_r.at[nz // 2])

    def z_block(n):
        pair = [block(z_dest(z_late[slot]), 2 * sub_c) for slot in (2 * n, 2 * n + 1)]
        both = mm(jnp.concatenate([s_hi[rows, :] for rows in pair]), scaled[...], NT)
        moved = both[:, 0:D] + both[:, D:2 * D]
        moved = moved + mm(jnp.concatenate([s_lo[rows, :] for rows in pair]), scaled[0:D, :], NT)
        for place, rows in enumerate(pair):
            zp[rows, :] = moved[2 * sub_c * place:2 * sub_c * (place + 1)]
        for slot in (2 * n, 2 * n + 1):
            to_partner(zp, zp_pair, slot, z_late[slot], late_s.at[n], late_r.at[n])

    for n in range(nz // 2 - 1):
        z_block(n)
        if n > 1:
            z_forward(n - 2)
    fill_column(2, target_adj)
    sx[...] = sx[...] * cols[2]
    if nz // 2 > 2:
        z_forward(nz // 2 - 3)

    arrived(7, nc)
    source_adj = sc_ref[...] - total_of(7, nc)

    coef[...] = rho * source_adj
    scale_points(xt, xt2)
    tall_r = cb * sub_r
    for n in range(ch_r):
        rows = block(lax.rem(r // cb + r_list[n * cb][0], ch_r), tall_r)
        both = mm(rt_hi[rows, :], xt2[...], NT)
        moved = both[:, 0:D] + both[:, D:2 * D] + mm(rt_lo[rows, :], xt2[0:D, :], NT)
        acc = rt[rows, 0:128] * coef[0:1, :]
        for q in range(1, groups):
            acc = acc + rt[rows, q * 128:(q + 1) * 128] * coef[q:q + 1, :]
        tp[rows, :] = y_ref[rows, :] * jnp.sum(acc, axis=1, keepdims=True) - moved - sx[rows, :]
        for slot in range(n * cb, (n + 1) * cb):
            if slot < nr - 1:
                along_r(tp, tp_recv, slot, *r_list[slot], late_s.at[nz // 2 + 1], late_r.at[nz // 2 + 1])
        if n == 0:
            z_block(nz // 2 - 1)
            z_forward(nz // 2 - 2)
        if n == ch_r - 1:
            z_forward(nz // 2 - 1)

    fill_column(1, source_adj)
    own_c, own_r = block(c, sub_c), block(r, sub_r)
    wait_bytes(ry_recv.at[pl.ds(0, cut)], bulk_r.at[1])
    wait_bytes(ry_recv.at[pl.ds(cut, nz - 1 - cut)], bulk_r.at[2])
    moved = ry_send[nz - 1]
    for slot in range(nz - 1):
        moved = moved + ry_recv[slot]
    wait_bytes(zp_recv, late_r.at[nz // 2])
    late = zp_send[nz - 1]
    for slot in range(nz - 1):
        late = late + zp_recv[slot]
    out_ref[0:sub_c, :] = x_ref[own_c, :] * cols[0, own_c, :] - cols[1, own_c, :] * moved - late
    wait_bytes(tp_recv, late_r.at[nz // 2 + 1])
    late = tp[own_r, :]
    for slot in range(nr - 1):
        late = late + tp_recv[slot]
    out_ref[sub_c:sub_c + sub_r, :] = cols[2, own_r, :] * y_ref[own_r, :] + late

    for slot, n in enumerate((nc, nr, nr, nc, nr, nc, nr, nc)):
        wait_bytes(recv.at[slot, pl.ds(0, n - 1)], ssem.at[slot])
    wait_bytes(ry_pair, bulk_s.at[0])
    wait_bytes(ry_recv.at[pl.ds(0, cut)], bulk_s.at[1])
    wait_bytes(ry_recv.at[pl.ds(cut, nz - 1 - cut)], bulk_s.at[2])
    for n in range(nz // 2):
        wait_bytes(zp_pair.at[pl.ds(2 * n, 2)], late_s.at[n])
    wait_bytes(zp_recv, late_s.at[nz // 2])
    wait_bytes(tp_recv, late_s.at[nz // 2 + 1])


def shards(nr, nc, cb, lane_chunk, pieces, x, y, f, g, sc, tc):
    size = x.shape[0]
    groups = size // 128
    sub_r, sub_c = size // nr, size // nc
    vectors = [v.reshape(groups, 128) for v in (f, g, sc, tc)]
    vmem = pl.BlockSpec(memory_space=pltpu.VMEM)
    peers = max(nr, nc) - 1
    nz = nc // 2
    square = (size, size)
    both = pl.pallas_call(
        functools.partial(kernel, nr, nc, cb, lane_chunk, pieces),
        out_shape=jax.ShapeDtypeStruct((sub_c + sub_r, D), F32),
        in_specs=[vmem] * 6,
        out_specs=vmem,
        scratch_shapes=[
            pltpu.VMEM((size, 4 * D), BF16),
            pltpu.VMEM((size, 4 * D), BF16),
            pltpu.VMEM(square, F32),
            pltpu.VMEM(square, F32),
            pltpu.VMEM(square, BF16),
            pltpu.VMEM(square, BF16),
            pltpu.VMEM(square, BF16),
            pltpu.VMEM(square, BF16),
            pltpu.VMEM((D, size), F32),
            pltpu.VMEM((D, size), F32),
            pltpu.VMEM((2 * D, size), BF16),
            pltpu.VMEM((2 * D, size), BF16),
            pltpu.VMEM((2 * D, size), BF16),
            pltpu.VMEM((2, groups, 128), F32),
            pltpu.VMEM((groups, 128), F32),
            pltpu.VMEM((8, groups, 128), F32),
            pltpu.VMEM((8, peers, groups, 128), F32),
            pltpu.SemaphoreType.DMA((8,)),
            pltpu.SemaphoreType.DMA((8,)),
            pltpu.VMEM((size, D), F32),
            pltpu.VMEM((nz, sub_c, D), F32),
            pltpu.VMEM((nz, sub_c, D), F32),
            pltpu.VMEM((nz - 1, sub_c, D), F32),
            pltpu.VMEM((size, D), F32),
            pltpu.VMEM((size, D), F32),
            pltpu.VMEM((nz, sub_c, D), F32),
            pltpu.VMEM((nz, sub_c, D), F32),
            pltpu.VMEM((nz - 1, sub_c, D), F32),
            pltpu.VMEM((size, D), F32),
            pltpu.VMEM((nr - 1, sub_r, D), F32),
            pltpu.VMEM((3, size, D), F32),
            pltpu.SemaphoreType.DMA((3,)),
            pltpu.SemaphoreType.DMA((3,)),
            pltpu.SemaphoreType.DMA((nz // 2 + 2,)),
            pltpu.SemaphoreType.DMA((nz // 2 + 2,)),
        ],
        compiler_params=pltpu.CompilerParams(
            collective_id=0, has_side_effects=True, vmem_limit_bytes=62 << 20
        ),
    )(x, y, *vectors)
    return both[:sub_c], both[sub_c:]


def solution(mesh, cb=4, lane_chunk=256, pieces=1):
    in_specs = (P("row", None), P("col", None), P("row"), P("col"), P("row"), P("col"))
    out_specs = (P(("row", "col"), None), P(("col", "row"), None))
    body = functools.partial(shards, mesh.shape["row"], mesh.shape["col"], cb, lane_chunk, pieces)
    return jax.shard_map(body, mesh=mesh, in_specs=in_specs, out_specs=out_specs, check_vma=False)
```
